128 devices in a mesh: wide: 32 (over x, z, core), narrow: 4 (over y).
Axes of the slice: x: 4, y: 4, z: 4, core: 2. Of those that a mesh axis runs over, the one named last changes fastest.
Arguments:
- points: bfloat16 [4, 512, 8, 512], P('narrow', 'wide'), may hold values from -1.5 to 1.5
- charges: bfloat16 [4, 512, 32, 512], P('narrow', 'wide'), may hold values from -6 to 6
- leaf_interp_basis: bfloat16 [4, 512, 512, 128], P('narrow', 'wide'), may hold values from -0.25 to 0.25
- leaf_skeleton: int32 [4, 512, 128], P('narrow', 'wide'), may hold values from 0 to 511, as said below
- local_transfer: bfloat16 [4, 480, 256, 128], P('narrow', 'wide'), may hold values from -0.5 to 0.5
- local_skeleton: int32 [4, 480, 128], P('narrow', 'wide'), may hold values from 0 to 255, as said below
- top_transfer: bfloat16 [4, 31, 256, 128], P('narrow'), may hold values from -0.5 to 0.5
- top_skeleton: int32 [4, 31, 128], P('narrow'), may hold values from 0 to 255, as said below
- near_list: int32 [4, 512, 8], P('narrow', 'wide'), may hold values from 0 to 511, as said below
- far_list: int32 [4, 32, 4], P('narrow', 'wide'), may hold values from 0 to 127, as said below
Outputs:
- potentials: bfloat16 [4, 512, 32, 512], P('narrow', 'wide')
The draws below stay inside these ranges and needn't reach their ends.
Inputs may be any that keep to these rules, and one draw needn't show every extreme that they name: `leaf_skeleton`: each row names 128 different points of its leaf. `local_skeleton`: each row names 128 different columns of the children's joined skeletons. `top_skeleton`: each row names 128 different columns of the children's joined skeletons. `near_list`: the row of leaf m starts with m and holds 8 different leaves of the same group, each within 16 of m. `far_list`: each row names 4 different device nodes; the first is the node of the row's own group at position (i + 16) mod 32 for row position i, the others belong to other groups.
All inputs are finite; a program needn't handle non-finite values.
Results may differ from the reference program's by a relative error of at most 0.00205.
Values may be sent and summed in bfloat16 or wider, within the bound.
A program may use at most 64 MiB of HBM per device.

```python
import math
import jax
import jax.numpy as jnp
from jax import lax

D = 8
BOX = 512
SKEL = 128
RHS = 32
NEAR = 8
FAR = 4
DEVICE_LEAVES = 16
GLEAVES = 512
N_WIDE = 32
N_NARROW = 4


def draw_points(key, part):
    shape = (N_NARROW, N_WIDE * DEVICE_LEAVES, D, BOX)
    values = 0.5 * jax.random.normal(jax.random.fold_in(key, 22), shape, jnp.float32)
    return jnp.clip(values, -1.5, 1.5).astype(jnp.bfloat16)


def distinct_picks(key, row_count, pool, wanted):
    scores = jax.random.randint(key, (row_count, pool), 0, 1 << 20) * pool + jnp.arange(pool)[None, :]
    return lax.top_k(scores, wanted)[1].astype(jnp.int32)


def draw_leaf_skeleton(key, part):
    picks = distinct_picks(jax.random.fold_in(key, 11), N_NARROW * N_WIDE * DEVICE_LEAVES, BOX, SKEL)
    return picks.reshape(N_NARROW, N_WIDE * DEVICE_LEAVES, SKEL)


def draw_local_skeleton(key, part):
    picks = distinct_picks(jax.random.fold_in(key, 12), N_NARROW * N_WIDE * (DEVICE_LEAVES - 1), 2 * SKEL, SKEL)
    return picks.reshape(N_NARROW, N_WIDE * (DEVICE_LEAVES - 1), SKEL)


def draw_top_skeleton(key, part):
    picks = distinct_picks(jax.random.fold_in(key, 13), N_NARROW * (N_WIDE - 1), 2 * SKEL, SKEL)
    return picks.reshape(N_NARROW, N_WIDE - 1, SKEL)


def draw_near_list(key, part):
    total = N_WIDE * DEVICE_LEAVES
    span = 2 * DEVICE_LEAVES + 1
    offsets = jnp.arange(span) - DEVICE_LEAVES
    leaves = jnp.arange(total)[:, None]
    target = leaves + offsets[None, :]
    valid = (target >= 0) & (target < total) & (offsets[None, :] != 0)
    scores = jax.random.randint(jax.random.fold_in(key, 14), (N_NARROW, total, span), 0, 1 << 20) * span + jnp.arange(span)[None, None, :]
    scores = jnp.where(valid[None], scores, -1 - jnp.arange(span)[None, None, :])
    picked = lax.top_k(scores, NEAR - 1)[1]
    others = leaves[None] + offsets[picked]
    own = jnp.broadcast_to(leaves[None], (N_NARROW, total, 1))
    return jnp.concatenate([own, others], axis=2).astype(jnp.int32)


def draw_far_list(key, part):
    pool = (N_NARROW - 1) * N_WIDE
    picks = distinct_picks(jax.random.fold_in(key, 15), N_NARROW * N_WIDE, pool, FAR - 1).reshape(N_NARROW, N_WIDE, FAR - 1)
    groups = jnp.arange(N_NARROW)[:, None, None]
    partner = (groups + 1 + picks // N_WIDE) % N_NARROW
    others = partner * N_WIDE + picks % N_WIDE
    positions = jnp.arange(N_WIDE)[None, :, None]
    mirror = groups * N_WIDE + (positions + N_WIDE // 2) % N_WIDE
    mirror = jnp.broadcast_to(mirror, (N_NARROW, N_WIDE, 1))
    return jnp.concatenate([mirror, others], axis=2).astype(jnp.int32)


def level_of(rng, dims, split, low, top_value):
    factor_of = 1.0
    for dim, blocks in split:
        heights = jax.random.uniform(jax.random.fold_in(jax.random.fold_in(rng, 6), dim), (blocks,), jnp.float32, low / len(split), top_value / len(split))
        factor_of = factor_of * jnp.repeat(jnp.exp(heights), dims[dim] // blocks).reshape((-1,) + (1,) * (len(dims) - 1 - dim))
    return factor_of


def centred(key, dims, deviation, limit, cuts=(), dtype=jnp.bfloat16):
    array = jax.random.normal(key, dims, jnp.float32) * deviation
    if len(cuts) > 0:
        array = level_of(key, dims, cuts, -0.22, 0.18) * array
    return jnp.clip(array, min=-limit, max=limit).astype(dtype)


def setup_inputs(seed: int = 0) -> dict:
    streams_of = jax.random.split(jax.random.key(seed), 11)
    points = draw_points(jax.random.fold_in(streams_of[10], 71), 0)
    charges = centred(streams_of[1], (N_NARROW, GLEAVES, RHS, BOX), 1.0, 6.0, ((0, 4), (1, 32)))
    leaf_interp_basis = centred(streams_of[2], (N_NARROW, GLEAVES, BOX, SKEL), BOX ** -0.5, 0.25, ((0, 4), (1, 32)))
    leaf_skeleton = draw_leaf_skeleton(jax.random.fold_in(streams_of[10], 71), 0)
    local_transfer = centred(streams_of[4], (N_NARROW, N_WIDE * (DEVICE_LEAVES - 1), 2 * SKEL, SKEL), SKEL ** -0.5, 0.5, ((0, 4), (1, 32)))
    local_skeleton = draw_local_skeleton(jax.random.fold_in(streams_of[10], 71), 0)
    top_transfer = centred(streams_of[6], (N_NARROW, N_WIDE - 1, 2 * SKEL, SKEL), SKEL ** -0.5, 0.5, ((0, 4),))
    top_skeleton = draw_top_skeleton(jax.random.fold_in(streams_of[10], 71), 0)
    near_list = draw_near_list(jax.random.fold_in(streams_of[10], 71), 0)
    far_list = draw_far_list(jax.random.fold_in(streams_of[10], 71), 0)
    return {"points": points, "charges": charges, "leaf_interp_basis": leaf_interp_basis, "leaf_skeleton": leaf_skeleton, "local_transfer": local_transfer, "local_skeleton": local_skeleton, "top_transfer": top_transfer, "top_skeleton": top_skeleton, "near_list": near_list, "far_list": far_list}


inv_width = 1.5
topmost_level = lax.Precision.HIGHEST

def gaussian(source_points, target_points):
    cross = jnp.einsum('...dn,...dm->...nm', source_points, target_points, precision=topmost_level)
    source_sq = lax.optimization_barrier(jnp.sum(source_points * source_points, axis=-2))
    target_sq = lax.optimization_barrier(jnp.sum(target_points * target_points, axis=-2))
    return jnp.exp(-inv_width * (source_sq[..., :, None] + target_sq[..., None, :] - 2.0 * cross))

def merge_up(left_node, right_node, transfer, chosen, rhs_count):
    joined = jnp.concatenate([left_node, right_node], axis=2)
    charge_weight = jnp.einsum('mrt,mts->mrs', joined[:, :rhs_count], transfer.astype(jnp.float32), precision=topmost_level)
    coords = jnp.take_along_axis(joined[:, rhs_count:], chosen[:, None, :], axis=2)
    return jnp.concatenate([charge_weight, coords], axis=1)

def push_down(potential_field, transfer):
    parents = potential_field.shape[0]
    children = jnp.einsum('mrs,mts->mrt', potential_field, transfer.astype(jnp.float32), precision=topmost_level)
    children = children.reshape(parents, potential_field.shape[1], 2, potential_field.shape[2])
    return jnp.transpose(children, (0, 2, 1, 3)).reshape(2 * parents, potential_field.shape[1], potential_field.shape[2])

def near_field(coords, charge_rows, near_ids):

    def one_leaf(leaf_idx):
        chosen = near_ids[leaf_idx]
        source_points = jnp.transpose(coords[chosen], (1, 0, 2)).reshape(D, NEAR * BOX)
        source_charge = jnp.transpose(charge_rows[chosen], (1, 0, 2)).reshape(RHS, NEAR * BOX)
        kernel_block = gaussian(source_points, coords[leaf_idx]).astype(jnp.bfloat16)
        return jnp.dot(source_charge, kernel_block, preferred_element_type=jnp.float32)
    return lax.map(one_leaf, jnp.arange(coords.shape[0]).astype(jnp.int32))

def reference(points, charges, leaf_interp_basis, leaf_skeleton, local_transfer, local_skeleton, top_transfer, top_skeleton, near_list, far_list):
    local_levels = DEVICE_LEAVES.bit_length() - 1
    top_levels = N_WIDE.bit_length() - 1
    out_scale = 1.0 / math.sqrt(BOX)
    device_nodes = []
    group_roots = []
    for cluster_index in range(N_NARROW):
        coords = points[cluster_index].astype(jnp.float32)
        charge_weight = jnp.einsum('xqn,xna->xqa', charges[cluster_index].astype(jnp.float32), leaf_interp_basis[cluster_index].astype(jnp.float32))
        level_nodes = jnp.concatenate([charge_weight, jnp.take_along_axis(coords, leaf_skeleton[cluster_index][:, None, :], axis=2)], axis=1)
        tables = local_transfer[cluster_index].reshape(N_WIDE, DEVICE_LEAVES - 1, 2 * SKEL, SKEL)
        chosen = local_skeleton[cluster_index].reshape(N_WIDE, DEVICE_LEAVES - 1, SKEL)
        for section in range(local_levels):
            parents = DEVICE_LEAVES >> section + 1
            level_nodes = merge_up(level_nodes[0::2], level_nodes[1::2], tables[:, parents - 1:2 * parents - 1].reshape(N_WIDE * parents, 2 * SKEL, SKEL), chosen[:, parents - 1:2 * parents - 1].reshape(N_WIDE * parents, SKEL), RHS)
        device_nodes.append(level_nodes)
        for section in range(top_levels):
            parents = N_WIDE >> section + 1
            level_nodes = merge_up(level_nodes[0::2], level_nodes[1::2], top_transfer[cluster_index, parents - 1:2 * parents - 1], top_skeleton[cluster_index, parents - 1:2 * parents - 1], RHS)
        group_roots.append(level_nodes[0])
    every_node = jnp.concatenate(device_nodes, axis=0)
    all_roots = jnp.stack(group_roots)
    outputs = []
    for cluster_index in range(N_NARROW):
        own_nodes = device_nodes[cluster_index]
        sources = every_node[far_list[cluster_index]]
        kernel_block = gaussian(sources[:, :, RHS:], own_nodes[:, None, RHS:])
        far_nodes = jnp.einsum('wfrn,wfnm->wrm', sources[:, :, :RHS], kernel_block, precision=topmost_level)
        other_mask = (jnp.arange(N_NARROW) != cluster_index).astype(jnp.float32)
        root_kernel = gaussian(all_roots[:, RHS:], all_roots[cluster_index][None, RHS:])
        top_field = jnp.einsum('grn,gnm,g->rm', all_roots[:, :RHS], root_kernel, other_mask, precision=topmost_level)[None]
        for section in reversed(range(top_levels)):
            parents = N_WIDE >> section + 1
            top_field = push_down(top_field, top_transfer[cluster_index, parents - 1:2 * parents - 1])
        potential_field = top_field + far_nodes
        tables = local_transfer[cluster_index].reshape(N_WIDE, DEVICE_LEAVES - 1, 2 * SKEL, SKEL)
        for section in reversed(range(local_levels)):
            parents = DEVICE_LEAVES >> section + 1
            potential_field = push_down(potential_field, tables[:, parents - 1:2 * parents - 1].reshape(N_WIDE * parents, 2 * SKEL, SKEL))
        distant_output = jnp.einsum('vcp,vfp->vcf', potential_field, leaf_interp_basis[cluster_index].astype(jnp.float32), precision=topmost_level)
        coords = points[cluster_index].astype(jnp.float32)
        near_out = near_field(coords, charges[cluster_index], near_list[cluster_index])
        outputs.append(((near_out + distant_output) * out_scale).astype(jnp.bfloat16))
    return jnp.stack(outputs)
```

```python
import functools
import math

import jax
import jax.numpy as jnp
from jax import lax
from jax.experimental import pallas as pl
from jax.experimental.pallas import tpu as pltpu
from jax.sharding import PartitionSpec as P

F32 = jnp.float32
BF16 = jnp.bfloat16
MESH = pl.DeviceIdType.MESH
RATE = 1.5 * math.log2(math.e)
LAST_DIMS = (((1,), (1,)), ((), ()))
FIRST_DIMS = (((0,), (0,)), ((), ()))
VMEM_BYTES = 56 * 2**20


def dot(a, b, dims=(((1,), (0,)), ((), ()))):
    return lax.dot_general(a, b, dims, preferred_element_type=F32)


def split3(x):
    first = x.astype(BF16).astype(F32)
    rest = x - first
    second = rest.astype(BF16).astype(F32)
    return first, second, rest - second


def hi_lo(x):
    high = x.astype(BF16)
    return high, (x - high.astype(F32)).astype(BF16)


def tail_rows(parts, slots):
    row = lax.broadcasted_iota(jnp.int32, (8, parts[0].shape[1]), 0)
    ones = (row >= slots[1]) & (row < slots[1] + 3)
    rows = jnp.where(ones, 1.0, 0.0)
    for i, part in enumerate(parts):
        rows = jnp.where(row == slots[0] + i, part, rows)
    return rows


def source_rows(points):
    norm = -RATE * jnp.sum(points * points, axis=0, keepdims=True)
    return jnp.concatenate([*split3(2.0 * RATE * points), tail_rows(split3(norm), (0, 3))], axis=0)


def target_rows(points):
    norm = -RATE * jnp.sum(points * points, axis=0, keepdims=True)
    return jnp.concatenate([points, points, points, tail_rows(split3(norm), (3, 0))], axis=0)


def merge(left, right, transfer, chosen, rhs):
    skel = left.shape[1]
    joined = jnp.concatenate([left, right], axis=1)
    high, low = hi_lo(joined[:rhs])
    rows = jnp.concatenate([high, low, joined[rhs:].astype(BF16)], axis=0)
    index = lax.broadcasted_iota(jnp.int32, (2 * skel, skel), 0)
    table = jnp.where(index == chosen, 1.0, 0.0).astype(BF16)
    both = dot(rows, jnp.concatenate([transfer, table], axis=1))
    weight = both[:rhs, :skel] + both[rhs : 2 * rhs, :skel]
    return jnp.concatenate([weight, both[2 * rhs :, skel:]], axis=0)


def node_field(source, target, rhs):
    log_kernel = dot(
        source_rows(source[rhs:]).astype(BF16), target_rows(target).astype(BF16), FIRST_DIMS
    )
    kernel_high, kernel_low = hi_lo(jnp.exp2(log_kernel))
    high, low = hi_lo(source[:rhs])
    both = dot(jnp.concatenate([high, low], axis=0), kernel_high)
    return both[:rhs] + both[rhs:] + dot(high, kernel_low)


def times_transposed(field, matrix):
    rows = field.shape[0]
    both = dot(jnp.concatenate(hi_lo(field), axis=0), matrix, LAST_DIMS)
    return both[:rows] + both[rows:]


def up_kernel(
    points, charges, basis, leaf_skel, transfer, skel,
    node, own_near, points_low, points_high, charges_low, charges_high,
    nodes, sources, targets, kernel_a, kernel_b, send_sem, recv_sem,
):
    leaves, rhs, box = charges.shape
    skel_count = basis.shape[2]
    wide = lax.axis_size("wide")
    me = lax.axis_index("wide")
    right, left = lax.rem(me + 1, wide), lax.rem(me + wide - 1, wide)
    barrier = pltpu.get_barrier_semaphore()
    for other in (left, right):
        pl.semaphore_signal(barrier, inc=1, device_id={"wide": other}, device_id_type=MESH)
    pl.semaphore_wait(barrier, 2)
    copies = []
    for i, (src, dst, other) in enumerate(
        (
            (charges, charges_low, right),
            (charges, charges_high, left),
            (points, points_low, right),
            (points, points_high, left),
        )
    ):
        copies.append(
            pltpu.make_async_remote_copy(
                src_ref=src, dst_ref=dst, send_sem=send_sem.at[i], recv_sem=recv_sem.at[i],
                device_id={"wide": other}, device_id_type=MESH,
            )
        )
    for copy in copies:
        copy.start()

    step = 4

    def leaf_nodes(first, carry):
        for leaf in [first * step + i for i in range(step)]:
            spots = points[leaf]
            index = lax.broadcasted_iota(jnp.int32, (box, skel_count), 0)
            table = jnp.where(index == leaf_skel[pl.ds(leaf, 1), :], 1.0, 0.0).astype(BF16)
            weight = dot(charges[leaf], basis[leaf])
            coords = dot(spots, table)
            nodes[leaf] = jnp.concatenate([weight, coords], axis=0)
        return carry

    lax.fori_loop(0, leaves // step, leaf_nodes, 0)
    level = [nodes[leaf] for leaf in range(leaves)]
    while len(level) > 1:
        parents = len(level) // 2
        level = [
            merge(
                level[2 * p], level[2 * p + 1], transfer[parents - 1 + p],
                skel[parents - 1 + p : parents + p, :], rhs,
            )
            for p in range(parents)
        ]
    node[...] = level[0]

    def rows(leaf, carry):
        spots = points[leaf].astype(F32)
        sources[leaf] = source_rows(spots).T.astype(BF16)
        targets[leaf] = target_rows(spots).astype(BF16)
        return carry

    lax.fori_loop(0, leaves, rows, 0)

    def fill(leaf, buffer):
        buffer[...] = jnp.exp2(dot(sources[leaf], targets[leaf])).astype(BF16)

    fill(0, kernel_a)

    def two_leaves(pair, carry):
        fill(2 * pair + 1, kernel_b)
        own_near[2 * pair] = dot(charges[2 * pair], kernel_a[...])
        fill(lax.rem(2 * pair + 2, leaves), kernel_a)
        own_near[2 * pair + 1] = dot(charges[2 * pair + 1], kernel_b[...])
        return carry

    lax.fori_loop(0, leaves // 2, two_leaves, 0)
    for copy in copies:
        copy.wait()


def near_kernel(
    near_list, points_low, points, points_high, charges_low, charges, charges_high, own_near,
    near_out, near_charges, sources, targets, kernel_a, kernel_b, sem,
):
    leaves, _, box = points.shape
    near = near_list.shape[1]
    first_leaf = (lax.axis_index("wide") - 1) * leaves
    copies = [
        pltpu.make_async_copy(src, near_charges.at[pl.ds(i * leaves, leaves)], sem.at[i])
        for i, src in enumerate((charges_low, charges, charges_high))
    ]
    for copy in copies:
        copy.start()

    def rows(leaf, carry):
        for i, part in enumerate((points_low, points, points_high)):
            spots = part[leaf].astype(F32)
            sources[i * leaves + leaf] = source_rows(spots).T.astype(BF16)
            if i == 1:
                targets[leaf] = target_rows(spots).astype(BF16)
        return carry

    lax.fori_loop(0, leaves, rows, 0)
    for copy in copies:
        copy.wait()

    def fill(leaf, k, buffer):
        source = sources[near_list[leaf, k] - first_leaf]
        buffer[...] = jnp.exp2(dot(source, targets[leaf])).astype(BF16)

    fill(0, 1, kernel_a)

    def two_leaves(pair, carry):
        steps = [(2 * pair + i, k) for i in range(2) for k in range(1, near)]
        steps.append((lax.rem(2 * pair + 2, leaves), 1))
        total = None
        for i, (leaf, k) in enumerate(steps[:-1]):
            now, later = (kernel_a, kernel_b) if i % 2 == 0 else (kernel_b, kernel_a)
            fill(*steps[i + 1], later)
            part = dot(near_charges[near_list[leaf, k] - first_leaf], now[...])
            total = (own_near[leaf] if k == 1 else total) + part
            if k == near - 1:
                near_out[leaf] = total
        return carry

    lax.fori_loop(0, leaves // 2, two_leaves, 0)


def down_kernel(
    far_list, all_nodes, own_node, top_transfer, top_skel, transfer, basis, near_out,
    out, tree, roots, send_sem, recv_sem,
):
    leaves, rhs, box = near_out.shape
    skel_count = basis.shape[2]
    wide, groups = lax.axis_size("wide"), lax.axis_size("narrow")
    me, group = lax.axis_index("wide"), lax.axis_index("narrow")
    others = [lax.rem(group + d, groups) for d in range(1, groups)]
    barrier = pltpu.get_barrier_semaphore()
    for other in others:
        pl.semaphore_signal(barrier, inc=1, device_id={"narrow": other}, device_id_type=MESH)

    parents = wide // 2
    while parents >= 1:
        step = min(4, parents)
        base = parents - 1

        def level(first, carry, step=step, base=base, parents=parents):
            for p in [first * step + i for i in range(step)]:
                if parents == wide // 2:
                    left = all_nodes[2 * p * groups + group]
                    right = all_nodes[(2 * p + 1) * groups + group]
                else:
                    left, right = tree[2 * base + 1 + 2 * p], tree[2 * base + 2 + 2 * p]
                tree[base + p] = merge(
                    left, right, top_transfer[base + p], top_skel[pl.ds(base + p, 1), :], rhs
                )
            return carry

        if step == parents:
            level(0, 0)
        else:
            lax.fori_loop(0, parents // step, level, 0)
        parents //= 2

    pl.semaphore_wait(barrier, groups - 1)
    copies = [
        pltpu.make_async_remote_copy(
            src_ref=tree.at[0], dst_ref=roots.at[i], send_sem=send_sem.at[i],
            recv_sem=recv_sem.at[i], device_id={"narrow": other}, device_id_type=MESH,
        )
        for i, other in enumerate(others)
    ]
    for copy in copies:
        copy.start()
    target = own_node[...][rhs:]
    far = None
    for i in range(far_list.shape[1]):
        e = far_list[0, i]
        source = all_nodes[lax.rem(e, wide) * groups + lax.div(e, wide)]
        part = node_field(source, target, rhs)
        far = part if far is None else far + part
    for copy in copies:
        copy.wait()
    target = tree[0][rhs:]
    field = None
    for i in range(groups - 1):
        part = node_field(roots[i], target, rhs)
        field = part if field is None else field + part
    for section in reversed(range(wide.bit_length() - 1)):
        slot = (wide >> section + 1) - 1 + lax.div(me, 2 << section)
        side = lax.rem(lax.div(me, 1 << section), 2)
        start = pl.multiple_of(side * skel_count, skel_count)
        field = times_transposed(field, top_transfer[slot, pl.ds(start, skel_count), :])
    fields = [field + far]
    while len(fields) < leaves:
        parents = len(fields)
        both = [times_transposed(fields[p], transfer[parents - 1 + p]) for p in range(parents)]
        fields = [half for pair in both for half in (pair[:, :skel_count], pair[:, skel_count:])]
    scale = 1.0 / math.sqrt(box)
    for leaf in range(leaves):
        far_part = times_transposed(fields[leaf], basis[leaf])
        out[leaf] = ((near_out[leaf] + far_part) * scale).astype(BF16)


def shards(
    points, charges, leaf_interp_basis, leaf_skeleton, local_transfer, local_skeleton,
    top_transfer, top_skeleton, near_list, far_list,
):
    points, charges, basis = points[0], charges[0], leaf_interp_basis[0]
    leaves, dims, box = points.shape
    rhs, skel = charges.shape[1], basis.shape[2]
    groups, wide = lax.axis_size("narrow"), lax.axis_size("wide")
    near = near_list.shape[2]
    vmem = pl.BlockSpec(memory_space=pltpu.VMEM)
    smem = pl.BlockSpec(memory_space=pltpu.SMEM)
    anywhere = pl.BlockSpec(memory_space=pl.ANY)

    def shape(dtype, *dims):
        return jax.ShapeDtypeStruct(dims, dtype)

    def cost(blocks):
        return pl.CostEstimate(
            flops=blocks * 2 * box * box * 288, bytes_accessed=4 * 2**20,
            transcendentals=blocks * box * box,
        )

    kernel_pair = [pltpu.VMEM((box, box), BF16)] * 2
    node, own_near, points_low, points_high, charges_low, charges_high = pl.pallas_call(
        up_kernel,
        out_shape=(
            shape(F32, rhs + dims, skel), shape(F32, leaves, rhs, box),
            shape(BF16, *points.shape), shape(BF16, *points.shape),
            shape(BF16, *charges.shape), shape(BF16, *charges.shape),
        ),
        in_specs=[vmem] * 6,
        out_specs=(vmem, vmem, anywhere, anywhere, anywhere, anywhere),
        scratch_shapes=[
            pltpu.VMEM((leaves, rhs + dims, skel), F32),
            pltpu.VMEM((leaves, box, 32), BF16),
            pltpu.VMEM((leaves, 32, box), BF16),
            *kernel_pair,
            pltpu.SemaphoreType.DMA((4,)),
            pltpu.SemaphoreType.DMA((4,)),
        ],
        compiler_params=pltpu.CompilerParams(
            collective_id=0, has_side_effects=True, vmem_limit_bytes=VMEM_BYTES
        ),
        cost_estimate=cost(leaves),
        name="up",
    )(points, charges, basis, leaf_skeleton[0], local_transfer[0], local_skeleton[0])
    all_nodes = lax.all_gather(node[None], ("wide", "narrow"), axis=0, tiled=True)
    near_out = pl.pallas_call(
        near_kernel,
        out_shape=shape(F32, leaves, rhs, box),
        in_specs=[smem, vmem, vmem, vmem, anywhere, anywhere, anywhere, vmem],
        out_specs=vmem,
        scratch_shapes=[
            pltpu.VMEM((3 * leaves, rhs, box), BF16),
            pltpu.VMEM((3 * leaves, box, 32), BF16),
            pltpu.VMEM((leaves, 32, box), BF16),
            *kernel_pair,
            pltpu.SemaphoreType.DMA((3,)),
        ],
        compiler_params=pltpu.CompilerParams(vmem_limit_bytes=VMEM_BYTES),
        cost_estimate=cost(leaves * (near - 1)),
        name="near",
    )(
        near_list[0], points_low, points, points_high, charges_low, charges, charges_high, own_near
    )
    out = pl.pallas_call(
        down_kernel,
        out_shape=shape(BF16, leaves, rhs, box),
        in_specs=[smem] + [vmem] * 7,
        out_specs=vmem,
        scratch_shapes=[
            pltpu.VMEM((wide - 1, rhs + dims, skel), F32),
            pltpu.VMEM((groups - 1, rhs + dims, skel), F32),
            pltpu.SemaphoreType.DMA((groups - 1,)),
            pltpu.SemaphoreType.DMA((groups - 1,)),
        ],
        compiler_params=pltpu.CompilerParams(
            collective_id=1, has_side_effects=True, vmem_limit_bytes=VMEM_BYTES
        ),
        name="down",
    )(
        far_list[0], all_nodes, node, top_transfer[0], top_skeleton[0], local_transfer[0], basis,
        near_out,
    )
    return out[None]


def solution(mesh):
    return jax.shard_map(
        shards,
        mesh=mesh,
        in_specs=(
            P("narrow", "wide", None, None),
            P("narrow", "wide", None, None),
            P("narrow", "wide", None, None),
            P("narrow", "wide", None),
            P("narrow", "wide", None, None),
            P("narrow", "wide", None),
            P("narrow", None, None, None),
            P("narrow", None, None),
            P("narrow", "wide", None),
            P("narrow", "wide", None),
        ),
        out_specs=P("narrow", "wide", None, None),
        check_vma=False,
    )
```

```python
import functools
import math

import jax
import jax.numpy as jnp
from jax import lax
from jax.experimental import pallas as pl
from jax.experimental.pallas import tpu as pltpu
from jax.sharding import PartitionSpec as P

F32 = jnp.float32
BF16 = jnp.bfloat16
MESH = pl.DeviceIdType.MESH
RATE = 1.5 * math.log2(math.e)
LAST_DIMS = (((1,), (1,)), ((), ()))
FIRST_DIMS = (((0,), (0,)), ((), ()))
VMEM_BYTES = 56 * 2**20


def dot(a, b, dims=(((1,), (0,)), ((), ()))):
    return lax.dot_general(a, b, dims, preferred_element_type=F32)


def split3(x):
    first = x.astype(BF16).astype(F32)
    rest = x - first
    second = rest.astype(BF16).astype(F32)
    return first, second, rest - second


def hi_lo(x):
    high = x.astype(BF16)
    return high, (x - high.astype(F32)).astype(BF16)


def tail_rows(parts, slots):
    row = lax.broadcasted_iota(jnp.int32, (8, parts[0].shape[1]), 0)
    ones = (row >= slots[1]) & (row < slots[1] + 3)
    rows = jnp.where(ones, 1.0, 0.0)
    for i, part in enumerate(parts):
        rows = jnp.where(row == slots[0] + i, part, rows)
    return rows


def source_rows(points):
    norm = -RATE * jnp.sum(points * points, axis=0, keepdims=True)
    return jnp.concatenate([*split3(2.0 * RATE * points), tail_rows(split3(norm), (0, 3))], axis=0)


def target_rows(points):
    norm = -RATE * jnp.sum(points * points, axis=0, keepdims=True)
    return jnp.concatenate([points, points, points, tail_rows(split3(norm), (3, 0))], axis=0)


def merge(left, right, transfer, chosen, rhs):
    skel = left.shape[1]
    joined = jnp.concatenate([left, right], axis=1)
    high, low = hi_lo(joined[:rhs])
    rows = jnp.concatenate([high, low, joined[rhs:].astype(BF16)], axis=0)
    index = lax.broadcasted_iota(jnp.int32, (2 * skel, skel), 0)
    table = jnp.where(index == chosen, 1.0, 0.0).astype(BF16)
    both = dot(rows, jnp.concatenate([transfer, table], axis=1))
    weight = both[:rhs, :skel] + both[rhs : 2 * rhs, :skel]
    return jnp.concatenate([weight, both[2 * rhs :, skel:]], axis=0)


def node_field(source, target, rhs):
    log_kernel = dot(
        source_rows(source[rhs:]).astype(BF16), target_rows(target).astype(BF16), FIRST_DIMS
    )
    kernel_high, kernel_low = hi_lo(jnp.exp2(log_kernel))
    high, low = hi_lo(source[:rhs])
    both = dot(jnp.concatenate([high, low], axis=0), kernel_high)
    return both[:rhs] + both[rhs:] + dot(high, kernel_low)


def times_transposed(field, matrix):
    rows = field.shape[0]
    both = dot(jnp.concatenate(hi_lo(field), axis=0), matrix, LAST_DIMS)
    return both[:rows] + both[rows:]


def main_kernel(
    near_list, far_list, points, charges, basis, transfer, top_transfer, leaf_skel, skel, top_skel,
    field_out, near_out,
    near_points, near_charges, basis_here, transfer_here, top_here, nodes, all_nodes, tree, roots,
    sources, targets, kernel_a, kernel_b, local_sem, send_sem, recv_sem,
):
    leaves, rhs, box = charges.shape
    skel_count = basis.shape[2]
    near = near_list.shape[0]
    wide, groups = lax.axis_size("wide"), lax.axis_size("narrow")
    me, group = lax.axis_index("wide"), lax.axis_index("narrow")
    chips = wide // 2
    side = math.isqrt(chips)
    core, chip = lax.rem(me, 2), lax.div(me, 2)
    row, column = lax.div(chip, side), lax.rem(chip, side)
    right, left = lax.rem(me + 1, wide), lax.rem(me + wide - 1, wide)
    sibling = chip * 2 + 1 - core

    def in_row(step):
        return lax.rem(column + step, side)

    def in_column(step):
        return lax.rem(row + step, side)

    def in_groups(step):
        return lax.rem(group + step, groups)

    row_peers = [(row * side + in_row(d)) * 2 + core for d in range(1, side)]
    column_peers = [(in_column(d) * side + column) * 2 + core for d in range(1, side)]
    group_peers = [in_groups(d) for d in range(1, groups)]

    local = [
        pltpu.make_async_copy(src, dst, local_sem.at[i])
        for i, (src, dst) in enumerate(
            (
                (charges, near_charges.at[pl.ds(leaves, leaves)]),
                (points, near_points.at[1]),
                (basis, basis_here),
                (transfer, transfer_here),
                (top_transfer, top_here),
            )
        )
    ]
    for copy in local:
        copy.start()
    barrier = pltpu.get_barrier_semaphore()
    wide_peers = [right, left] + row_peers + column_peers
    for other in wide_peers:
        pl.semaphore_signal(barrier, inc=1, device_id={"wide": other}, device_id_type=MESH)
    for other in group_peers:
        pl.semaphore_signal(barrier, inc=1, device_id={"narrow": other}, device_id_type=MESH)
    pl.semaphore_wait(barrier, len(wide_peers) + len(group_peers))

    used = []

    def exchange(src, dst, device, incoming=None):
        i = len(used)
        used.append(i)
        sems = {"send_sem": send_sem.at[i], "recv_sem": recv_sem.at[i]}
        sent = pltpu.make_async_remote_copy(
            src_ref=src, dst_ref=dst, device_id=device, device_id_type=MESH, **sems
        )
        landed = dst if incoming is None else incoming
        got = pltpu.make_async_remote_copy(
            src_ref=landed, dst_ref=landed, device_id=device, device_id_type=MESH, **sems
        )
        sent.start()
        return sent, got

    def finish(pairs):
        for sent, got in pairs:
            sent.wait_send()
            got.wait_recv()

    halo = []
    for other, block, place in ((right, 0, 0), (left, 2, 2 * leaves)):
        halo.append(
            exchange(charges, near_charges.at[pl.ds(place, leaves)], {"wide": other})
        )
        halo.append(exchange(points, near_points.at[block], {"wide": other}))

    for copy in local[:3]:
        copy.wait()
    step = 4

    def leaf_nodes(first, carry):
        for leaf in [first * step + i for i in range(step)]:
            spots = near_points[1, leaf]
            index = lax.broadcasted_iota(jnp.int32, (box, skel_count), 0)
            table = jnp.where(index == leaf_skel[pl.ds(leaf, 1), :], 1.0, 0.0).astype(BF16)
            weight = dot(near_charges[leaves + leaf], basis_here[leaf])
            coords = dot(spots, table)
            nodes[leaf] = jnp.concatenate([weight, coords], axis=0)
        return carry

    lax.fori_loop(0, leaves // step, leaf_nodes, 0)
    local[3].wait()
    level = [nodes[leaf] for leaf in range(leaves)]
    while len(level) > 1:
        parents = len(level) // 2
        level = [
            merge(
                level[2 * p], level[2 * p + 1], transfer_here[parents - 1 + p],
                skel[parents - 1 + p], rhs,
            )
            for p in range(parents)
        ]
    half = core * chips
    slot = half + chip
    all_nodes[group, slot] = level[0]
    mine = all_nodes.at[group, slot]
    stage_a = [
        exchange(
            mine, mine, {"wide": other},
            all_nodes.at[group, half + row * side + in_row(side - d)],
        )
        for d, other in enumerate(row_peers, 1)
    ]

    def own_rows(leaf, carry):
        spots = near_points[1, leaf].astype(F32)
        sources[leaves + leaf] = source_rows(spots).T.astype(BF16)
        targets[leaf] = target_rows(spots).astype(BF16)
        return carry

    lax.fori_loop(0, leaves, own_rows, 0)

    def fill_own(leaf, buffer):
        buffer[...] = jnp.exp2(dot(sources[leaves + leaf], targets[leaf])).astype(BF16)

    def own_pair(pair, carry):
        fill_own(2 * pair + 1, kernel_b)
        near_out[2 * pair] = dot(near_charges[leaves + 2 * pair], kernel_a[...])
        fill_own(lax.rem(2 * pair + 2, leaves), kernel_a)
        near_out[2 * pair + 1] = dot(near_charges[leaves + 2 * pair + 1], kernel_b[...])
        return carry

    fill_own(0, kernel_a)
    lax.fori_loop(0, leaves // 4, own_pair, 0)
    finish(stage_a)
    line = all_nodes.at[group, pl.ds(half + row * side, side)]
    stage_b = [
        exchange(
            line, line, {"wide": other},
            all_nodes.at[group, pl.ds(half + in_column(side - d) * side, side)],
        )
        for d, other in enumerate(column_peers, 1)
    ]
    lax.fori_loop(leaves // 4, leaves // 2, own_pair, 0)
    finish(stage_b)
    plane = all_nodes.at[group, pl.ds(half, chips)]
    other_half = pl.ds((1 - core) * chips, chips)
    stage_d = [
        exchange(
            plane, plane, {"narrow": other},
            all_nodes.at[in_groups(groups - d), pl.ds(half, chips)],
        )
        for d, other in enumerate(group_peers, 1)
    ]
    stage_c = [exchange(plane, plane, {"wide": sibling}, all_nodes.at[group, other_half])]
    finish(halo)

    def halo_rows(leaf, carry):
        for block in (0, 2):
            spots = near_points[block, leaf].astype(F32)
            sources[block * leaves + leaf] = source_rows(spots).T.astype(BF16)
        return carry

    lax.fori_loop(0, leaves, halo_rows, 0)
    first_leaf = (me - 1) * leaves

    def place_of(leaf, k):
        return jnp.clip(near_list[k, leaf] - first_leaf, 0, 3 * leaves - 1)

    def fill(leaf, k, buffer):
        source = sources[place_of(leaf, k)]
        buffer[...] = jnp.exp2(dot(source, targets[leaf])).astype(BF16)

    def two_leaves(pair, carry):
        steps = [(2 * pair + i, k) for i in range(2) for k in range(1, near)]
        steps.append((lax.rem(2 * pair + 2, leaves), 1))
        total = None
        for i, (leaf, k) in enumerate(steps[:-1]):
            now, later = (kernel_a, kernel_b) if i % 2 == 0 else (kernel_b, kernel_a)
            fill(*steps[i + 1], later)
            part = dot(near_charges[place_of(leaf, k)], now[...])
            total = (near_out[leaf] if k == 1 else total) + part
            if k == near - 1:
                near_out[leaf] = total
        return carry

    fill(0, 1, kernel_a)
    lax.fori_loop(0, 2, two_leaves, 0)
    finish(stage_c)
    local[4].wait()

    parents = chips
    while parents >= 1:
        step = min(4, parents)
        base = parents - 1

        def level(first, carry, step=step, base=base, parents=parents):
            for p in [first * step + i for i in range(step)]:
                if parents == chips:
                    left, right = all_nodes[group, p], all_nodes[group, chips + p]
                else:
                    left, right = tree[2 * base + 1 + 2 * p], tree[2 * base + 2 + 2 * p]
                tree[base + p] = merge(left, right, top_here[base + p], top_skel[base + p], rhs)
            return carry

        if step == parents:
            level(0, 0)
        else:
            lax.fori_loop(0, parents // step, level, 0)
        parents //= 2
    stage_r = [
        exchange(tree.at[0], roots.at[d], {"narrow": other}) for d, other in enumerate(group_peers)
    ]
    lax.fori_loop(2, 5, two_leaves, 0)
    finish(stage_d)
    stage_e = []
    for d in range(1, groups):
        other = in_groups(d)
        block = all_nodes.at[other, pl.ds(half, chips)]
        stage_e.append(
            exchange(block, block, {"wide": sibling}, all_nodes.at[other, other_half])
        )
    finish(stage_r)
    target = tree[0][rhs:]
    field = None
    for i in range(groups - 1):
        part = node_field(roots[i], target, rhs)
        field = part if field is None else field + part
    for section in reversed(range(wide.bit_length() - 1)):
        place = (wide >> section + 1) - 1 + lax.div(me, 2 << section)
        start = lax.rem(lax.div(me, 1 << section), 2) * skel_count
        matrix = top_here[place, pl.ds(pl.multiple_of(start, skel_count), skel_count), :]
        field = times_transposed(field, matrix)
    field_out[...] = field
    lax.fori_loop(5, leaves // 2, two_leaves, 0)
    finish(stage_e)
    target = all_nodes[group, slot][rhs:]
    field = field_out[...]
    for i in range(far_list.shape[1]):
        e = far_list[0, i]
        place = lax.rem(e, wide)
        source = all_nodes[lax.div(e, wide), lax.rem(place, 2) * chips + lax.div(place, 2)]
        field = field + node_field(source, target, rhs)
    field_out[...] = field


def down_kernel(field, transfer, basis, near_out, out):
    leaves, rhs, box = near_out.shape
    skel_count = basis.shape[2]
    fields = [field[...]]
    while len(fields) < leaves:
        parents = len(fields)
        both = [times_transposed(fields[p], transfer[parents - 1 + p]) for p in range(parents)]
        fields = [half for pair in both for half in (pair[:, :skel_count], pair[:, skel_count:])]
    scale = 1.0 / math.sqrt(box)
    for leaf in range(leaves):
        far_part = times_transposed(fields[leaf], basis[leaf])
        out[leaf] = ((near_out[leaf] + far_part) * scale).astype(BF16)


def shards(
    points, charges, leaf_interp_basis, leaf_skeleton, local_transfer, local_skeleton,
    top_transfer, top_skeleton, near_list, far_list,
):
    points, charges, basis = points[0], charges[0], leaf_interp_basis[0]
    leaves, dims, box = points.shape
    rhs, skel = charges.shape[1], basis.shape[2]
    groups, wide = lax.axis_size("narrow"), lax.axis_size("wide")
    vmem = pl.BlockSpec(memory_space=pltpu.VMEM)
    smem = pl.BlockSpec(memory_space=pltpu.SMEM)
    anywhere = pl.BlockSpec(memory_space=pl.ANY)

    def shape(dtype, *dims):
        return jax.ShapeDtypeStruct(dims, dtype)

    size = (rhs + dims, skel)
    side = math.isqrt(wide // 2)
    copies = 4 + 2 * (side - 1) + 1 + 3 * (groups - 1)
    field, near_out = pl.pallas_call(
        main_kernel,
        out_shape=(shape(F32, rhs, skel), shape(F32, leaves, rhs, box)),
        in_specs=[smem] * 2 + [anywhere] * 5 + [vmem] * 3,
        out_specs=(vmem, vmem),
        scratch_shapes=[
            pltpu.VMEM((3, *points.shape), BF16),
            pltpu.VMEM((3 * leaves, rhs, box), BF16),
            pltpu.VMEM(basis.shape, BF16),
            pltpu.VMEM(local_transfer.shape[1:], BF16),
            pltpu.VMEM(top_transfer.shape[1:], BF16),
            pltpu.VMEM((leaves, *size), F32),
            pltpu.VMEM((groups, wide, *size), F32),
            pltpu.VMEM((wide - 1, *size), F32),
            pltpu.VMEM((groups - 1, *size), F32),
            pltpu.VMEM((3 * leaves, box, 32), BF16),
            pltpu.VMEM((leaves, 32, box), BF16),
            pltpu.VMEM((box, box), BF16),
            pltpu.VMEM((box, box), BF16),
            pltpu.SemaphoreType.DMA((5,)),
            pltpu.SemaphoreType.DMA((copies,)),
            pltpu.SemaphoreType.DMA((copies,)),
        ],
        compiler_params=pltpu.CompilerParams(
            collective_id=0, has_side_effects=True, vmem_limit_bytes=VMEM_BYTES
        ),
        name="main",
    )(
        near_list[0].T, far_list[0], points, charges, basis, local_transfer[0], top_transfer[0],
        leaf_skeleton[0], jnp.swapaxes(local_skeleton, 0, 1), jnp.swapaxes(top_skeleton, 0, 1),
    )
    out = pl.pallas_call(
        down_kernel,
        out_shape=shape(BF16, leaves, rhs, box),
        in_specs=[vmem] * 4,
        out_specs=vmem,
        compiler_params=pltpu.CompilerParams(vmem_limit_bytes=VMEM_BYTES),
        name="down",
    )(field, local_transfer[0], basis, near_out)
    return out[None]


def solution(mesh):
    return jax.shard_map(
        shards,
        mesh=mesh,
        in_specs=(
            P("narrow", "wide", None, None),
            P("narrow", "wide", None, None),
            P("narrow", "wide", None, None),
            P("narrow", "wide", None),
            P("narrow", "wide", None, None),
            P("narrow", "wide", None),
            P("narrow", None, None, None),
            P("narrow", None, None),
            P("narrow", "wide", None),
            P("narrow", "wide", None),
        ),
        out_specs=P("narrow", "wide", None, None),
        check_vma=False,
    )
```

```python
import functools
import math

import jax
import jax.numpy as jnp
from jax import lax
from jax.experimental import pallas as pl
from jax.experimental.pallas import tpu as pltpu
from jax.sharding import PartitionSpec as P

F32 = jnp.float32
BF16 = jnp.bfloat16
MESH = pl.DeviceIdType.MESH
RATE = 1.5 * math.log2(math.e)
LAST_DIMS = (((1,), (1,)), ((), ()))
FIRST_DIMS = (((0,), (0,)), ((), ()))
VMEM_BYTES = 56 * 2**20


def dot(a, b, dims=(((1,), (0,)), ((), ()))):
    return lax.dot_general(a, b, dims, preferred_element_type=F32)


def split3(x):
    first = x.astype(BF16).astype(F32)
    rest = x - first
    second = rest.astype(BF16).astype(F32)
    return first, second, rest - second


def hi_lo(x):
    high = x.astype(BF16)
    return high, (x - high.astype(F32)).astype(BF16)


def tail_rows(parts, slots):
    row = lax.broadcasted_iota(jnp.int32, (8, parts[0].shape[1]), 0)
    ones = (row >= slots[1]) & (row < slots[1] + 3)
    rows = jnp.where(ones, 1.0, 0.0)
    for i, part in enumerate(parts):
        rows = jnp.where(row == slots[0] + i, part, rows)
    return rows


def source_rows(points):
    norm = -RATE * jnp.sum(points * points, axis=0, keepdims=True)
    return jnp.concatenate([*split3(2.0 * RATE * points), tail_rows(split3(norm), (0, 3))], axis=0)


def target_rows(points):
    norm = -RATE * jnp.sum(points * points, axis=0, keepdims=True)
    return jnp.concatenate([points, points, points, tail_rows(split3(norm), (3, 0))], axis=0)


def merge(left, right, transfer, chosen, rhs):
    skel = left.shape[1]
    joined = jnp.concatenate([left, right], axis=1)
    high, low = hi_lo(joined[:rhs])
    rows = jnp.concatenate([high, low, joined[rhs:].astype(BF16)], axis=0)
    index = lax.broadcasted_iota(jnp.int32, (2 * skel, skel), 0)
    table = jnp.where(index == chosen, 1.0, 0.0).astype(BF16)
    both = dot(rows, jnp.concatenate([transfer, table], axis=1))
    weight = both[:rhs, :skel] + both[rhs : 2 * rhs, :skel]
    return jnp.concatenate([weight, both[2 * rhs :, skel:]], axis=0)


def node_field(source, target, rhs):
    log_kernel = dot(
        source_rows(source[rhs:]).astype(BF16), target_rows(target).astype(BF16), FIRST_DIMS
    )
    kernel_high, kernel_low = hi_lo(jnp.exp2(log_kernel))
    high, low = hi_lo(source[:rhs])
    both = dot(jnp.concatenate([high, low], axis=0), kernel_high)
    return both[:rhs] + both[rhs:] + dot(high, kernel_low)


def times_transposed(field, matrix):
    rows = field.shape[0]
    both = dot(jnp.concatenate(hi_lo(field), axis=0), matrix, LAST_DIMS)
    return both[:rows] + both[rows:]


def main_kernel(
    near_list, far_list, points, charges, basis, transfer, top_transfer, leaf_skel, skel, top_skel,
    field_out, near_out,
    near_points, near_charges, basis_here, transfer_here, top_here, nodes, all_nodes, tree, roots,
    sources, targets, kernel_a, kernel_b, local_sem, send_sem, recv_sem,
):
    leaves, rhs, box = charges.shape
    skel_count = basis.shape[2]
    near = near_list.shape[0]
    wide, groups = lax.axis_size("wide"), lax.axis_size("narrow")
    me, group = lax.axis_index("wide"), lax.axis_index("narrow")
    chips = wide // 2
    side = math.isqrt(chips)
    core, chip = lax.rem(me, 2), lax.div(me, 2)
    row, column = lax.div(chip, side), lax.rem(chip, side)
    right, left = lax.rem(me + 1, wide), lax.rem(me + wide - 1, wide)
    sibling = chip * 2 + 1 - core

    def in_row(step):
        return lax.rem(column + step, side)

    def in_column(step):
        return lax.rem(row + step, side)

    def in_groups(step):
        return lax.rem(group + step, groups)

    row_peers = [(row * side + in_row(d)) * 2 + core for d in range(1, side)]
    column_peers = [(in_column(d) * side + column) * 2 + core for d in range(1, side)]
    group_peers = [in_groups(d) for d in range(1, groups)]

    local = [
        pltpu.make_async_copy(src, dst, local_sem.at[i])
        for i, (src, dst) in enumerate(
            (
                (charges, near_charges.at[pl.ds(leaves, leaves)]),
                (points, near_points.at[1]),
                (basis, basis_here),
                (transfer, transfer_here),
                (top_transfer, top_here),
            )
        )
    ]
    for copy in local:
        copy.start()
    barrier = pltpu.get_barrier_semaphore()
    wide_peers = [right, left] + row_peers + column_peers
    for other in wide_peers:
        pl.semaphore_signal(barrier, inc=1, device_id={"wide": other}, device_id_type=MESH)
    for other in group_peers:
        pl.semaphore_signal(barrier, inc=1, device_id={"narrow": other}, device_id_type=MESH)
    pl.semaphore_wait(barrier, len(wide_peers) + len(group_peers))

    used = []

    def exchange(src, dst, device, incoming=None):
        i = len(used)
        used.append(i)
        sems = {"send_sem": send_sem.at[i], "recv_sem": recv_sem.at[i]}
        sent = pltpu.make_async_remote_copy(
            src_ref=src, dst_ref=dst, device_id=device, device_id_type=MESH, **sems
        )
        landed = dst if incoming is None else incoming
        got = pltpu.make_async_remote_copy(
            src_ref=landed, dst_ref=landed, device_id=device, device_id_type=MESH, **sems
        )
        sent.start()
        return sent, got

    def finish(pairs):
        for sent, got in pairs:
            sent.wait_send()
            got.wait_recv()

    sides = ((right, 0), (left, 2))
    halo_points = [exchange(points, near_points.at[b], {"wide": other}) for other, b in sides]
    halo_charges = [
        exchange(charges, near_charges.at[pl.ds(b * leaves, leaves)], {"wide": other})
        for other, b in sides
    ]

    for copy in local[:3]:
        copy.wait()
    step = 4

    def leaf_nodes(first, carry):
        for leaf in [first * step + i for i in range(step)]:
            spots = near_points[1, leaf]
            index = lax.broadcasted_iota(jnp.int32, (box, skel_count), 0)
            table = jnp.where(index == leaf_skel[pl.ds(leaf, 1), :], 1.0, 0.0).astype(BF16)
            weight = dot(near_charges[leaves + leaf], basis_here[leaf])
            coords = dot(spots, table)
            nodes[leaf] = jnp.concatenate([weight, coords], axis=0)
        return carry

    lax.fori_loop(0, leaves // step, leaf_nodes, 0)
    local[3].wait()
    level = [nodes[leaf] for leaf in range(leaves)]
    while len(level) > 1:
        parents = len(level) // 2
        level = [
            merge(
                level[2 * p], level[2 * p + 1], transfer_here[parents - 1 + p],
                skel[parents - 1 + p], rhs,
            )
            for p in range(parents)
        ]
    half = core * chips
    slot = half + chip
    all_nodes[group, slot] = level[0]
    mine = all_nodes.at[group, slot]
    stage_a = [
        exchange(
            mine, mine, {"wide": other},
            all_nodes.at[group, half + row * side + in_row(side - d)],
        )
        for d, other in enumerate(row_peers, 1)
    ]

    finish(halo_points)

    def fill_own(leaf, buffer):
        spots = near_points[1, leaf].astype(F32)
        source = source_rows(spots).T.astype(BF16)
        target = target_rows(spots).astype(BF16)
        sources[leaves + leaf] = source
        targets[leaf] = target
        buffer[...] = jnp.exp2(dot(source, target)).astype(BF16)

    def own_pair(pair, carry):
        for i, (now, later) in enumerate(((kernel_a, kernel_b), (kernel_b, kernel_a))):
            leaf = 2 * pair + i
            fill_own(lax.rem(leaf + 1, leaves), later)
            near_out[leaf] = dot(near_charges[leaves + leaf], now[...])
            for block in (0, 2):
                spots = near_points[block, leaf].astype(F32)
                sources[block * leaves + leaf] = source_rows(spots).T.astype(BF16)
        return carry

    fill_own(0, kernel_a)
    lax.fori_loop(0, leaves // 2, own_pair, 0)
    finish(stage_a)
    line = all_nodes.at[group, pl.ds(half + row * side, side)]
    stage_b = [
        exchange(
            line, line, {"wide": other},
            all_nodes.at[group, pl.ds(half + in_column(side - d) * side, side)],
        )
        for d, other in enumerate(column_peers, 1)
    ]
    finish(halo_charges)
    first_leaf = (me - 1) * leaves

    def place_of(leaf, k):
        return jnp.clip(near_list[k, leaf] - first_leaf, 0, 3 * leaves - 1)

    def fill(leaf, k, buffer):
        source = sources[place_of(leaf, k)]
        buffer[...] = jnp.exp2(dot(source, targets[leaf])).astype(BF16)

    def two_leaves(pair, carry):
        steps = [(2 * pair + i, k) for i in range(2) for k in range(1, near)]
        steps.append((lax.rem(2 * pair + 2, leaves), 1))
        total = None
        for i, (leaf, k) in enumerate(steps[:-1]):
            now, later = (kernel_a, kernel_b) if i % 2 == 0 else (kernel_b, kernel_a)
            fill(*steps[i + 1], later)
            part = dot(near_charges[place_of(leaf, k)], now[...])
            total = (near_out[leaf] if k == 1 else total) + part
            if k == near - 1:
                near_out[leaf] = total
        return carry

    fill(0, 1, kernel_a)
    lax.fori_loop(0, 1, two_leaves, 0)
    finish(stage_b)
    plane = all_nodes.at[group, pl.ds(half, chips)]
    other_half = pl.ds((1 - core) * chips, chips)
    stage_d = [
        exchange(
            plane, plane, {"narrow": other},
            all_nodes.at[in_groups(groups - d), pl.ds(half, chips)],
        )
        for d, other in enumerate(group_peers, 1)
    ]
    stage_c = [exchange(plane, plane, {"wide": sibling}, all_nodes.at[group, other_half])]
    lax.fori_loop(1, 3, two_leaves, 0)
    finish(stage_c)
    local[4].wait()

    parents = chips
    while parents >= 1:
        step = min(4, parents)
        base = parents - 1

        def level(first, carry, step=step, base=base, parents=parents):
            for p in [first * step + i for i in range(step)]:
                if parents == chips:
                    left, right = all_nodes[group, p], all_nodes[group, chips + p]
                else:
                    left, right = tree[2 * base + 1 + 2 * p], tree[2 * base + 2 + 2 * p]
                tree[base + p] = merge(left, right, top_here[base + p], top_skel[base + p], rhs)
            return carry

        if step == parents:
            level(0, 0)
        else:
            lax.fori_loop(0, parents // step, level, 0)
        parents //= 2
    stage_r = [
        exchange(tree.at[0], roots.at[d], {"narrow": other}) for d, other in enumerate(group_peers)
    ]
    lax.fori_loop(3, 6, two_leaves, 0)
    finish(stage_d)
    stage_e = []
    for d in range(1, groups):
        other = in_groups(d)
        block = all_nodes.at[other, pl.ds(half, chips)]
        stage_e.append(
            exchange(block, block, {"wide": sibling}, all_nodes.at[other, other_half])
        )
    finish(stage_r)
    target = tree[0][rhs:]
    field = None
    for i in range(groups - 1):
        part = node_field(roots[i], target, rhs)
        field = part if field is None else field + part
    for section in reversed(range(wide.bit_length() - 1)):
        place = (wide >> section + 1) - 1 + lax.div(me, 2 << section)
        start = lax.rem(lax.div(me, 1 << section), 2) * skel_count
        matrix = top_here[place, pl.ds(pl.multiple_of(start, skel_count), skel_count), :]
        field = times_transposed(field, matrix)
    field_out[...] = field
    lax.fori_loop(6, leaves // 2, two_leaves, 0)
    finish(stage_e)
    target = all_nodes[group, slot][rhs:]
    field = field_out[...]
    for i in range(far_list.shape[1]):
        e = far_list[0, i]
        place = lax.rem(e, wide)
        source = all_nodes[lax.div(e, wide), lax.rem(place, 2) * chips + lax.div(place, 2)]
        field = field + node_field(source, target, rhs)
    field_out[...] = field


def down_kernel(
    field, transfer, basis, near_out, out, transfer_here, basis_here, near_here, sem
):
    leaves, rhs, box = near_out.shape
    skel_count = basis.shape[2]
    copies = [
        pltpu.make_async_copy(src, dst, sem.at[i])
        for i, (src, dst) in enumerate(
            ((transfer, transfer_here), (basis, basis_here), (near_out, near_here))
        )
    ]
    for copy in copies:
        copy.start()
    copies[0].wait()
    fields = [field[...]]
    while len(fields) < leaves:
        parents = len(fields)
        both = [times_transposed(fields[p], transfer_here[parents - 1 + p]) for p in range(parents)]
        fields = [half for pair in both for half in (pair[:, :skel_count], pair[:, skel_count:])]
    copies[1].wait()
    copies[2].wait()
    scale = 1.0 / math.sqrt(box)
    for leaf in range(leaves):
        far_part = times_transposed(fields[leaf], basis_here[leaf])
        out[leaf] = ((near_here[leaf] + far_part) * scale).astype(BF16)


def shards(
    points, charges, leaf_interp_basis, leaf_skeleton, local_transfer, local_skeleton,
    top_transfer, top_skeleton, near_list, far_list,
):
    points, charges, basis = points[0], charges[0], leaf_interp_basis[0]
    leaves, dims, box = points.shape
    rhs, skel = charges.shape[1], basis.shape[2]
    groups, wide = lax.axis_size("narrow"), lax.axis_size("wide")
    vmem = pl.BlockSpec(memory_space=pltpu.VMEM)
    smem = pl.BlockSpec(memory_space=pltpu.SMEM)
    anywhere = pl.BlockSpec(memory_space=pl.ANY)

    def shape(dtype, *dims):
        return jax.ShapeDtypeStruct(dims, dtype)

    size = (rhs + dims, skel)
    side = math.isqrt(wide // 2)
    copies = 4 + 2 * (side - 1) + 1 + 3 * (groups - 1)
    field, near_out = pl.pallas_call(
        main_kernel,
        out_shape=(shape(F32, rhs, skel), shape(F32, leaves, rhs, box)),
        in_specs=[smem] * 2 + [anywhere] * 5 + [vmem] * 3,
        out_specs=(vmem, vmem),
        scratch_shapes=[
            pltpu.VMEM((3, *points.shape), BF16),
            pltpu.VMEM((3 * leaves, rhs, box), BF16),
            pltpu.VMEM(basis.shape, BF16),
            pltpu.VMEM(local_transfer.shape[1:], BF16),
            pltpu.VMEM(top_transfer.shape[1:], BF16),
            pltpu.VMEM((leaves, *size), F32),
            pltpu.VMEM((groups, wide, *size), F32),
            pltpu.VMEM((wide - 1, *size), F32),
            pltpu.VMEM((groups - 1, *size), F32),
            pltpu.VMEM((3 * leaves, box, 32), BF16),
            pltpu.VMEM((leaves, 32, box), BF16),
            pltpu.VMEM((box, box), BF16),
            pltpu.VMEM((box, box), BF16),
            pltpu.SemaphoreType.DMA((5,)),
            pltpu.SemaphoreType.DMA((copies,)),
            pltpu.SemaphoreType.DMA((copies,)),
        ],
        compiler_params=pltpu.CompilerParams(
            collective_id=0, has_side_effects=True, vmem_limit_bytes=VMEM_BYTES
        ),
        name="main",
    )(
        near_list[0].T, far_list[0], points, charges, basis, local_transfer[0], top_transfer[0],
        leaf_skeleton[0], jnp.swapaxes(local_skeleton, 0, 1), jnp.swapaxes(top_skeleton, 0, 1),
    )
    out = pl.pallas_call(
        down_kernel,
        out_shape=shape(BF16, leaves, rhs, box),
        in_specs=[vmem] + [anywhere] * 3,
        out_specs=vmem,
        scratch_shapes=[
            pltpu.VMEM(local_transfer.shape[1:], BF16),
            pltpu.VMEM(basis.shape, BF16),
            pltpu.VMEM((leaves, rhs, box), F32),
            pltpu.SemaphoreType.DMA((3,)),
        ],
        compiler_params=pltpu.CompilerParams(vmem_limit_bytes=VMEM_BYTES),
        name="down",
    )(field, local_transfer[0], basis, near_out)
    return out[None]


def solution(mesh):
    return jax.shard_map(
        shards,
        mesh=mesh,
        in_specs=(
            P("narrow", "wide", None, None),
            P("narrow", "wide", None, None),
            P("narrow", "wide", None, None),
            P("narrow", "wide", None),
            P("narrow", "wide", None, None),
            P("narrow", "wide", None),
            P("narrow", None, None, None),
            P("narrow", None, None),
            P("narrow", "wide", None),
            P("narrow", "wide", None),
        ),
        out_specs=P("narrow", "wide", None, None),
        check_vma=False,
    )
```

```python
import functools
import math

import jax
import jax.numpy as jnp
from jax import lax
from jax.experimental import pallas as pl
from jax.experimental.pallas import tpu as pltpu
from jax.sharding import PartitionSpec as P

F32 = jnp.float32
BF16 = jnp.bfloat16
MESH = pl.DeviceIdType.MESH
RATE = 1.5 * math.log2(math.e)
LAST_DIMS = (((1,), (1,)), ((), ()))
FIRST_DIMS = (((0,), (0,)), ((), ()))
VMEM_BYTES = 56 * 2**20


def dot(a, b, dims=(((1,), (0,)), ((), ()))):
    return lax.dot_general(a, b, dims, preferred_element_type=F32)


def split3(x):
    first = x.astype(BF16).astype(F32)
    rest = x - first
    second = rest.astype(BF16).astype(F32)
    return first, second, rest - second


def hi_lo(x):
    high = x.astype(BF16)
    return high, (x - high.astype(F32)).astype(BF16)


def tail_rows(parts, slots):
    row = lax.broadcasted_iota(jnp.int32, (8, parts[0].shape[1]), 0)
    ones = (row >= slots[1]) & (row < slots[1] + 3)
    rows = jnp.where(ones, 1.0, 0.0)
    for i, part in enumerate(parts):
        rows = jnp.where(row == slots[0] + i, part, rows)
    return rows


def source_rows(points):
    norm = -RATE * jnp.sum(points * points, axis=0, keepdims=True)
    return jnp.concatenate([*split3(2.0 * RATE * points), tail_rows(split3(norm), (0, 3))], axis=0)


def target_rows(points):
    norm = -RATE * jnp.sum(points * points, axis=0, keepdims=True)
    return jnp.concatenate([points, points, points, tail_rows(split3(norm), (3, 0))], axis=0)


def merge(left, right, transfer, chosen, rhs):
    skel = left.shape[1]
    joined = jnp.concatenate([left, right], axis=1)
    high, low = hi_lo(joined[:rhs])
    rows = jnp.concatenate([high, low, joined[rhs:].astype(BF16)], axis=0)
    index = lax.broadcasted_iota(jnp.int32, (2 * skel, skel), 0)
    table = jnp.where(index == chosen, 1.0, 0.0).astype(BF16)
    both = dot(rows, jnp.concatenate([transfer, table], axis=1))
    weight = both[:rhs, :skel] + both[rhs : 2 * rhs, :skel]
    return jnp.concatenate([weight, both[2 * rhs :, skel:]], axis=0)


def node_field(source, target, rhs):
    log_kernel = dot(
        source_rows(source[rhs:]).astype(BF16), target_rows(target).astype(BF16), FIRST_DIMS
    )
    kernel_high, kernel_low = hi_lo(jnp.exp2(log_kernel))
    high, low = hi_lo(source[:rhs])
    both = dot(jnp.concatenate([high, low], axis=0), kernel_high)
    return both[:rhs] + both[rhs:] + dot(high, kernel_low)


def times_transposed(field, matrix):
    rows = field.shape[0]
    both = dot(jnp.concatenate(hi_lo(field), axis=0), matrix, LAST_DIMS)
    return both[:rows] + both[rows:]


def main_kernel(
    near_list, far_list, points, charges, basis, transfer, top_transfer, leaf_skel, skel, top_skel,
    out,
    near_out, near_points, near_charges, basis_here, transfer_here, top_here, nodes, all_nodes, tree, roots, top_field,
    sources, targets, kernel_a, kernel_b, local_sem, send_sem, recv_sem,
):
    leaves, rhs, box = charges.shape
    skel_count = basis.shape[2]
    near = near_list.shape[0]
    wide, groups = lax.axis_size("wide"), lax.axis_size("narrow")
    me, group = lax.axis_index("wide"), lax.axis_index("narrow")
    chips = wide // 2
    side = math.isqrt(chips)
    core, chip = lax.rem(me, 2), lax.div(me, 2)
    row, column = lax.div(chip, side), lax.rem(chip, side)
    right, left = lax.rem(me + 1, wide), lax.rem(me + wide - 1, wide)
    sibling = chip * 2 + 1 - core

    def in_row(step):
        return lax.rem(column + step, side)

    def in_column(step):
        return lax.rem(row + step, side)

    def in_groups(step):
        return lax.rem(group + step, groups)

    row_peers = [(row * side + in_row(d)) * 2 + core for d in range(1, side)]
    column_peers = [(in_column(d) * side + column) * 2 + core for d in range(1, side)]
    group_peers = [in_groups(d) for d in range(1, groups)]

    local = [
        pltpu.make_async_copy(src, dst, local_sem.at[i])
        for i, (src, dst) in enumerate(
            (
                (charges, near_charges.at[pl.ds(leaves, leaves)]),
                (points, near_points.at[1]),
                (basis, basis_here),
                (transfer, transfer_here),
                (top_transfer, top_here),
            )
        )
    ]
    for copy in local:
        copy.start()
    barrier = pltpu.get_barrier_semaphore()
    wide_peers = [right, left] + row_peers + column_peers
    for other in wide_peers:
        pl.semaphore_signal(barrier, inc=1, device_id={"wide": other}, device_id_type=MESH)
    for other in group_peers:
        pl.semaphore_signal(barrier, inc=1, device_id={"narrow": other}, device_id_type=MESH)
    pl.semaphore_wait(barrier, len(wide_peers) + len(group_peers))

    used = []

    def exchange(src, dst, device, incoming=None):
        i = len(used)
        used.append(i)
        sems = {"send_sem": send_sem.at[i], "recv_sem": recv_sem.at[i]}
        sent = pltpu.make_async_remote_copy(
            src_ref=src, dst_ref=dst, device_id=device, device_id_type=MESH, **sems
        )
        landed = dst if incoming is None else incoming
        got = pltpu.make_async_remote_copy(
            src_ref=landed, dst_ref=landed, device_id=device, device_id_type=MESH, **sems
        )
        sent.start()
        return sent, got

    def finish(pairs):
        for sent, got in pairs:
            sent.wait_send()
            got.wait_recv()

    sides = ((right, 0), (left, 2))
    halo_points = [exchange(points, near_points.at[b], {"wide": other}) for other, b in sides]
    halo_charges = [
        exchange(charges, near_charges.at[pl.ds(b * leaves, leaves)], {"wide": other})
        for other, b in sides
    ]

    for copy in local[:3]:
        copy.wait()
    step = 4

    def leaf_nodes(first, carry):
        for leaf in [first * step + i for i in range(step)]:
            spots = near_points[1, leaf]
            index = lax.broadcasted_iota(jnp.int32, (box, skel_count), 0)
            table = jnp.where(index == leaf_skel[pl.ds(leaf, 1), :], 1.0, 0.0).astype(BF16)
            weight = dot(near_charges[leaves + leaf], basis_here[leaf])
            coords = dot(spots, table)
            nodes[leaf] = jnp.concatenate([weight, coords], axis=0)
        return carry

    lax.fori_loop(0, leaves // step, leaf_nodes, 0)
    local[3].wait()
    level = [nodes[leaf] for leaf in range(leaves)]
    while len(level) > 1:
        parents = len(level) // 2
        level = [
            merge(
                level[2 * p], level[2 * p + 1], transfer_here[parents - 1 + p],
                skel[parents - 1 + p], rhs,
            )
            for p in range(parents)
        ]
    half = core * chips
    slot = half + chip
    all_nodes[group, slot] = level[0]
    mine = all_nodes.at[group, slot]
    stage_a = [
        exchange(
            mine, mine, {"wide": other},
            all_nodes.at[group, half + row * side + in_row(side - d)],
        )
        for d, other in enumerate(row_peers, 1)
    ]


    def fill_own(leaf, buffer):
        spots = near_points[1, leaf].astype(F32)
        source = source_rows(spots).T.astype(BF16)
        target = target_rows(spots).astype(BF16)
        sources[leaves + leaf] = source
        targets[leaf] = target
        buffer[...] = jnp.exp2(dot(source, target)).astype(BF16)

    def own_pair(pair, carry):
        for i, (now, later) in enumerate(((kernel_a, kernel_b), (kernel_b, kernel_a))):
            leaf = 2 * pair + i
            fill_own(lax.rem(leaf + 1, leaves), later)
            near_out[leaf] = dot(near_charges[leaves + leaf], now[...])
        return carry

    def own_pair_and_halo(pair, carry):
        own_pair(pair, carry)
        for leaf in [(pair - leaves // 4) * 4 + i for i in range(4)]:
            for block in (0, 2):
                spots = near_points[block, leaf].astype(F32)
                sources[block * leaves + leaf] = source_rows(spots).T.astype(BF16)
        return carry

    fill_own(0, kernel_a)
    lax.fori_loop(0, leaves // 4, own_pair, 0)
    finish(halo_points)
    lax.fori_loop(leaves // 4, 3 * leaves // 8, own_pair_and_halo, 0)
    finish(stage_a)
    line = all_nodes.at[group, pl.ds(half + row * side, side)]
    stage_b = [
        exchange(
            line, line, {"wide": other},
            all_nodes.at[group, pl.ds(half + in_column(side - d) * side, side)],
        )
        for d, other in enumerate(column_peers, 1)
    ]
    lax.fori_loop(3 * leaves // 8, leaves // 2, own_pair_and_halo, 0)
    finish(halo_charges)
    first_leaf = (me - 1) * leaves

    def place_of(leaf, k):
        return jnp.clip(near_list[k, leaf] - first_leaf, 0, 3 * leaves - 1)

    def fill(leaf, k, buffer):
        source = sources[place_of(leaf, k)]
        buffer[...] = jnp.exp2(dot(source, targets[leaf])).astype(BF16)

    def two_leaves(pair, carry):
        steps = [(2 * pair + i, k) for i in range(2) for k in range(1, near)]
        steps.append((lax.rem(2 * pair + 2, leaves), 1))
        total = None
        for i, (leaf, k) in enumerate(steps[:-1]):
            now, later = (kernel_a, kernel_b) if i % 2 == 0 else (kernel_b, kernel_a)
            fill(*steps[i + 1], later)
            part = dot(near_charges[place_of(leaf, k)], now[...])
            total = (near_out[leaf] if k == 1 else total) + part
            if k == near - 1:
                near_out[leaf] = total
        return carry

    fill(0, 1, kernel_a)
    lax.fori_loop(0, 2, two_leaves, 0)
    finish(stage_b)
    plane = all_nodes.at[group, pl.ds(half, chips)]
    other_half = pl.ds((1 - core) * chips, chips)
    stage_d = [
        exchange(
            plane, plane, {"narrow": other},
            all_nodes.at[in_groups(groups - d), pl.ds(half, chips)],
        )
        for d, other in enumerate(group_peers, 1)
    ]
    stage_c = [exchange(plane, plane, {"wide": sibling}, all_nodes.at[group, other_half])]
    lax.fori_loop(2, 4, two_leaves, 0)
    finish(stage_c)
    local[4].wait()

    parents = chips
    while parents >= 1:
        step = min(4, parents)
        base = parents - 1

        def level(first, carry, step=step, base=base, parents=parents):
            for p in [first * step + i for i in range(step)]:
                if parents == chips:
                    left, right = all_nodes[group, p], all_nodes[group, chips + p]
                else:
                    left, right = tree[2 * base + 1 + 2 * p], tree[2 * base + 2 + 2 * p]
                tree[base + p] = merge(left, right, top_here[base + p], top_skel[base + p], rhs)
            return carry

        if step == parents:
            level(0, 0)
        else:
            lax.fori_loop(0, parents // step, level, 0)
        parents //= 2
    stage_r = [
        exchange(tree.at[0], roots.at[d], {"narrow": other}) for d, other in enumerate(group_peers)
    ]

    def pass_on(d):
        other = in_groups(groups - d)
        block = all_nodes.at[other, pl.ds(half, chips)]
        mirrored = all_nodes.at[other, other_half]
        return exchange(block, block, {"wide": sibling}, mirrored)

    close = [d for d in range(1, groups) if d in (1, groups - 1)]
    distant = [d for d in range(1, groups) if d not in close]
    lax.fori_loop(4, 5, two_leaves, 0)
    finish([stage_d[d - 1] for d in close])
    stage_e = [pass_on(d) for d in close]
    lax.fori_loop(5, 7, two_leaves, 0)
    finish([stage_d[d - 1] for d in distant])
    stage_e += [pass_on(d) for d in distant]
    finish(stage_r)
    target = tree[0][rhs:]
    field = None
    for i in range(groups - 1):
        part = node_field(roots[i], target, rhs)
        field = part if field is None else field + part
    for section in reversed(range(wide.bit_length() - 1)):
        place = (wide >> section + 1) - 1 + lax.div(me, 2 << section)
        start = lax.rem(lax.div(me, 1 << section), 2) * skel_count
        matrix = top_here[place, pl.ds(pl.multiple_of(start, skel_count), skel_count), :]
        field = times_transposed(field, matrix)
    top_field[...] = field
    lax.fori_loop(7, leaves // 2, two_leaves, 0)
    finish(stage_e)
    target = all_nodes[group, slot][rhs:]
    field = top_field[...]
    for i in range(far_list.shape[1]):
        e = far_list[0, i]
        place = lax.rem(e, wide)
        source = all_nodes[lax.div(e, wide), lax.rem(place, 2) * chips + lax.div(place, 2)]
        field = field + node_field(source, target, rhs)
    fields = [field]
    while len(fields) < leaves:
        parents = len(fields)
        both = [times_transposed(fields[p], transfer_here[parents - 1 + p]) for p in range(parents)]
        fields = [half for pair in both for half in (pair[:, :skel_count], pair[:, skel_count:])]
    scale = 1.0 / math.sqrt(box)
    for leaf in range(leaves):
        far_part = times_transposed(fields[leaf], basis_here[leaf])
        out[leaf] = ((near_out[leaf] + far_part) * scale).astype(BF16)


def shards(
    points, charges, leaf_interp_basis, leaf_skeleton, local_transfer, local_skeleton,
    top_transfer, top_skeleton, near_list, far_list,
):
    points, charges, basis = points[0], charges[0], leaf_interp_basis[0]
    leaves, dims, box = points.shape
    rhs, skel = charges.shape[1], basis.shape[2]
    groups, wide = lax.axis_size("narrow"), lax.axis_size("wide")
    vmem = pl.BlockSpec(memory_space=pltpu.VMEM)
    smem = pl.BlockSpec(memory_space=pltpu.SMEM)
    anywhere = pl.BlockSpec(memory_space=pl.ANY)

    def shape(dtype, *dims):
        return jax.ShapeDtypeStruct(dims, dtype)

    size = (rhs + dims, skel)
    side = math.isqrt(wide // 2)
    copies = 4 + 2 * (side - 1) + 1 + 3 * (groups - 1)
    out = pl.pallas_call(
        main_kernel,
        out_shape=shape(BF16, leaves, rhs, box),
        in_specs=[smem] * 2 + [anywhere] * 5 + [vmem] * 3,
        out_specs=vmem,
        scratch_shapes=[
            pltpu.VMEM((leaves, rhs, box), F32),
            pltpu.VMEM((3, *points.shape), BF16),
            pltpu.VMEM((3 * leaves, rhs, box), BF16),
            pltpu.VMEM(basis.shape, BF16),
            pltpu.VMEM(local_transfer.shape[1:], BF16),
            pltpu.VMEM(top_transfer.shape[1:], BF16),
            pltpu.VMEM((leaves, *size), F32),
            pltpu.VMEM((groups, wide, *size), F32),
            pltpu.VMEM((wide - 1, *size), F32),
            pltpu.VMEM((groups - 1, *size), F32),
            pltpu.VMEM((rhs, skel), F32),
            pltpu.VMEM((3 * leaves, box, 32), BF16),
            pltpu.VMEM((leaves, 32, box), BF16),
            pltpu.VMEM((box, box), BF16),
            pltpu.VMEM((box, box), BF16),
            pltpu.SemaphoreType.DMA((5,)),
            pltpu.SemaphoreType.DMA((copies,)),
            pltpu.SemaphoreType.DMA((copies,)),
        ],
        compiler_params=pltpu.CompilerParams(
            collective_id=0, has_side_effects=True, vmem_limit_bytes=VMEM_BYTES
        ),
        name="main",
    )(
        near_list[0].T, far_list[0], points, charges, basis, local_transfer[0], top_transfer[0],
        leaf_skeleton[0], jnp.swapaxes(local_skeleton, 0, 1), jnp.swapaxes(top_skeleton, 0, 1),
    )
    return out[None]


def solution(mesh):
    return jax.shard_map(
        shards,
        mesh=mesh,
        in_specs=(
            P("narrow", "wide", None, None),
            P("narrow", "wide", None, None),
            P("narrow", "wide", None, None),
            P("narrow", "wide", None),
            P("narrow", "wide", None, None),
            P("narrow", "wide", None),
            P("narrow", None, None, None),
            P("narrow", None, None),
            P("narrow", "wide", None),
            P("narrow", "wide", None),
        ),
        out_specs=P("narrow", "wide", None, None),
        check_vma=False,
    )
```

```python
import functools
import math

import jax
import jax.numpy as jnp
from jax import lax
from jax.experimental import pallas as pl
from jax.experimental.pallas import tpu as pltpu
from jax.sharding import PartitionSpec as P

F32 = jnp.float32
BF16 = jnp.bfloat16
MESH = pl.DeviceIdType.MESH
RATE = 1.5 * math.log2(math.e)
LAST_DIMS = (((1,), (1,)), ((), ()))
FIRST_DIMS = (((0,), (0,)), ((), ()))
VMEM_BYTES = 56 * 2**20


def dot(a, b, dims=(((1,), (0,)), ((), ()))):
    return lax.dot_general(a, b, dims, preferred_element_type=F32)


def split3(x):
    first = x.astype(BF16).astype(F32)
    rest = x - first
    second = rest.astype(BF16).astype(F32)
    return first, second, rest - second


def hi_lo(x):
    high = x.astype(BF16)
    return high, (x - high.astype(F32)).astype(BF16)


def tail_rows(parts, slots):
    row = lax.broadcasted_iota(jnp.int32, (8, parts[0].shape[1]), 0)
    ones = (row >= slots[1]) & (row < slots[1] + 3)
    rows = jnp.where(ones, 1.0, 0.0)
    for i, part in enumerate(parts):
        rows = jnp.where(row == slots[0] + i, part, rows)
    return rows


def source_rows(points):
    norm = -RATE * jnp.sum(points * points, axis=0, keepdims=True)
    return jnp.concatenate([*split3(2.0 * RATE * points), tail_rows(split3(norm), (0, 3))], axis=0)


def target_rows(points):
    norm = -RATE * jnp.sum(points * points, axis=0, keepdims=True)
    return jnp.concatenate([points, points, points, tail_rows(split3(norm), (3, 0))], axis=0)


def merge(left, right, transfer, chosen, rhs):
    skel = left.shape[1]
    joined = jnp.concatenate([left, right], axis=1)
    high, low = hi_lo(joined[:rhs])
    rows = jnp.concatenate([high, low, joined[rhs:].astype(BF16)], axis=0)
    index = lax.broadcasted_iota(jnp.int32, (2 * skel, skel), 0)
    table = jnp.where(index == chosen, 1.0, 0.0).astype(BF16)
    both = dot(rows, jnp.concatenate([transfer, table], axis=1))
    weight = both[:rhs, :skel] + both[rhs : 2 * rhs, :skel]
    return jnp.concatenate([weight, both[2 * rhs :, skel:]], axis=0)


def node_field(source, target, rhs):
    log_kernel = dot(
        source_rows(source[rhs:]).astype(BF16), target_rows(target).astype(BF16), FIRST_DIMS
    )
    kernel_high, kernel_low = hi_lo(jnp.exp2(log_kernel))
    high, low = hi_lo(source[:rhs])
    both = dot(jnp.concatenate([high, low], axis=0), kernel_high)
    return both[:rhs] + both[rhs:] + dot(high, kernel_low)


def times_transposed(field, matrix):
    rows = field.shape[0]
    both = dot(jnp.concatenate(hi_lo(field), axis=0), matrix, LAST_DIMS)
    return both[:rows] + both[rows:]


def main_kernel(
    near_list, far_list, points, charges, basis, transfer, top_transfer, leaf_skel, skel, top_skel,
    out,
    near_out, near_points, near_charges, basis_here, transfer_here, top_here, nodes, all_nodes, tree, roots, top_field,
    sources, targets, kernel_a, kernel_b, local_sem, send_sem, recv_sem,
):
    leaves, rhs, box = charges.shape
    skel_count = basis.shape[2]
    near = near_list.shape[0]
    wide, groups = lax.axis_size("wide"), lax.axis_size("narrow")
    me, group = lax.axis_index("wide"), lax.axis_index("narrow")
    chips = wide // 2
    side = math.isqrt(chips)
    core, chip = lax.rem(me, 2), lax.div(me, 2)
    row, column = lax.div(chip, side), lax.rem(chip, side)
    right, left = lax.rem(me + 1, wide), lax.rem(me + wide - 1, wide)
    sibling = chip * 2 + 1 - core

    def in_row(step):
        return lax.rem(column + step, side)

    def in_column(step):
        return lax.rem(row + step, side)

    def in_groups(step):
        return lax.rem(group + step, groups)

    row_peers = [(row * side + in_row(d)) * 2 + core for d in range(1, side)]
    column_peers = [(in_column(d) * side + column) * 2 + core for d in range(1, side)]
    group_peers = [in_groups(d) for d in range(1, groups)]

    local = [
        pltpu.make_async_copy(src, dst, local_sem.at[i])
        for i, (src, dst) in enumerate(
            (
                (charges, near_charges.at[pl.ds(leaves, leaves)]),
                (points, near_points.at[1]),
                (basis, basis_here),
                (transfer, transfer_here),
                (top_transfer, top_here),
            )
        )
    ]
    for copy in local:
        copy.start()
    barrier = pltpu.get_barrier_semaphore()
    wide_peers = [right, left] + row_peers + column_peers
    for other in wide_peers:
        pl.semaphore_signal(barrier, inc=1, device_id={"wide": other}, device_id_type=MESH)
    for other in group_peers:
        pl.semaphore_signal(barrier, inc=1, device_id={"narrow": other}, device_id_type=MESH)
    pl.semaphore_wait(barrier, len(wide_peers) + len(group_peers))

    used = []

    def exchange(src, dst, device, incoming=None):
        i = len(used)
        used.append(i)
        sems = {"send_sem": send_sem.at[i], "recv_sem": recv_sem.at[i]}
        sent = pltpu.make_async_remote_copy(
            src_ref=src, dst_ref=dst, device_id=device, device_id_type=MESH, **sems
        )
        landed = dst if incoming is None else incoming
        got = pltpu.make_async_remote_copy(
            src_ref=landed, dst_ref=landed, device_id=device, device_id_type=MESH, **sems
        )
        sent.start()
        return sent, got

    def finish(pairs):
        for sent, got in pairs:
            sent.wait_send()
            got.wait_recv()

    sides = ((right, 0), (left, 2))
    halo_points = [exchange(points, near_points.at[b], {"wide": other}) for other, b in sides]
    halo_charges = [
        exchange(charges, near_charges.at[pl.ds(b * leaves, leaves)], {"wide": other})
        for other, b in sides
    ]

    for copy in local[:3]:
        copy.wait()
    step = 4

    def leaf_nodes(first, carry):
        for leaf in [first * step + i for i in range(step)]:
            spots = near_points[1, leaf]
            index = lax.broadcasted_iota(jnp.int32, (box, skel_count), 0)
            table = jnp.where(index == leaf_skel[pl.ds(leaf, 1), :], 1.0, 0.0).astype(BF16)
            weight = dot(near_charges[leaves + leaf], basis_here[leaf])
            coords = dot(spots, table)
            nodes[leaf] = jnp.concatenate([weight, coords], axis=0)
        return carry

    lax.fori_loop(0, leaves // step, leaf_nodes, 0)
    local[3].wait()
    level = [nodes[leaf] for leaf in range(leaves)]
    while len(level) > 1:
        parents = len(level) // 2
        level = [
            merge(
                level[2 * p], level[2 * p + 1], transfer_here[parents - 1 + p],
                skel[parents - 1 + p], rhs,
            )
            for p in range(parents)
        ]
    half = core * chips
    slot = half + chip
    all_nodes[group, slot] = level[0]
    mine = all_nodes.at[group, slot]
    stage_a = [
        exchange(
            mine, mine, {"wide": other},
            all_nodes.at[group, half + row * side + in_row(side - d)],
        )
        for d, other in enumerate(row_peers, 1)
    ]


    def fill_own(leaf, buffer):
        spots = near_points[1, leaf].astype(F32)
        source = source_rows(spots).T.astype(BF16)
        target = target_rows(spots).astype(BF16)
        sources[leaves + leaf] = source
        targets[leaf] = target
        buffer[...] = jnp.exp2(dot(source, target)).astype(BF16)

    def own_pair(pair, carry):
        for i, (now, later) in enumerate(((kernel_a, kernel_b), (kernel_b, kernel_a))):
            leaf = 2 * pair + i
            fill_own(lax.rem(leaf + 1, leaves), later)
            near_out[leaf] = dot(near_charges[leaves + leaf], now[...])
        return carry

    def own_pair_and_halo(pair, carry):
        own_pair(pair, carry)
        for leaf in [(pair - leaves // 4) * 4 + i for i in range(4)]:
            for block in (0, 2):
                spots = near_points[block, leaf].astype(F32)
                sources[block * leaves + leaf] = source_rows(spots).T.astype(BF16)
        return carry

    fill_own(0, kernel_a)
    lax.fori_loop(0, leaves // 4, own_pair, 0)
    finish(halo_points)
    lax.fori_loop(leaves // 4, 3 * leaves // 8, own_pair_and_halo, 0)
    finish(stage_a)
    line = all_nodes.at[group, pl.ds(half + row * side, side)]
    stage_b = [
        exchange(
            line, line, {"wide": other},
            all_nodes.at[group, pl.ds(half + in_column(side - d) * side, side)],
        )
        for d, other in enumerate(column_peers, 1)
    ]
    lax.fori_loop(3 * leaves // 8, leaves // 2, own_pair_and_halo, 0)
    finish(halo_charges)
    first_leaf = (me - 1) * leaves

    def place_of(leaf, k):
        return jnp.clip(near_list[k, leaf] - first_leaf, 0, 3 * leaves - 1)

    def fill(leaf, k, buffer):
        source = sources[place_of(leaf, k)]
        buffer[...] = jnp.exp2(dot(source, targets[leaf])).astype(BF16)

    def two_leaves(pair, carry):
        steps = [(2 * pair + i, k) for i in range(2) for k in range(1, near)]
        steps.append((lax.rem(2 * pair + 2, leaves), 1))
        total = None
        for i, (leaf, k) in enumerate(steps[:-1]):
            now, later = (kernel_a, kernel_b) if i % 2 == 0 else (kernel_b, kernel_a)
            fill(*steps[i + 1], later)
            part = dot(near_charges[place_of(leaf, k)], now[...])
            total = (near_out[leaf] if k == 1 else total) + part
            if k == near - 1:
                near_out[leaf] = total
        return carry

    fill(0, 1, kernel_a)
    lax.fori_loop(0, 2, two_leaves, 0)
    finish(stage_b)
    plane = all_nodes.at[group, pl.ds(half, chips)]
    other_half = pl.ds((1 - core) * chips, chips)
    stage_d = [
        exchange(
            plane, plane, {"narrow": other},
            all_nodes.at[in_groups(groups - d), pl.ds(half, chips)],
        )
        for d, other in enumerate(group_peers, 1)
    ]
    stage_c = [exchange(plane, plane, {"wide": sibling}, all_nodes.at[group, other_half])]
    lax.fori_loop(2, 4, two_leaves, 0)
    finish(stage_c)
    local[4].wait()

    parents = chips
    while parents >= 1:
        step = min(4, parents)
        base = parents - 1

        def level(first, carry, step=step, base=base, parents=parents):
            for p in [first * step + i for i in range(step)]:
                if parents == chips:
                    left, right = all_nodes[group, p], all_nodes[group, chips + p]
                else:
                    left, right = tree[2 * base + 1 + 2 * p], tree[2 * base + 2 + 2 * p]
                tree[base + p] = merge(left, right, top_here[base + p], top_skel[base + p], rhs)
            return carry

        if step == parents:
            level(0, 0)
        else:
            lax.fori_loop(0, parents // step, level, 0)
        parents //= 2
    stage_r = [
        exchange(tree.at[0], roots.at[d], {"narrow": other}) for d, other in enumerate(group_peers)
    ]

    def pass_on(d):
        other = in_groups(groups - d)
        block = all_nodes.at[other, pl.ds(half, chips)]
        mirrored = all_nodes.at[other, other_half]
        return exchange(block, block, {"wide": sibling}, mirrored)

    lax.fori_loop(4, 7, two_leaves, 0)
    finish(stage_d)
    stage_e = [pass_on(d) for d in range(1, groups)]
    finish(stage_r)
    target = tree[0][rhs:]
    field = None
    for i in range(groups - 1):
        part = node_field(roots[i], target, rhs)
        field = part if field is None else field + part
    for section in reversed(range(wide.bit_length() - 1)):
        place = (wide >> section + 1) - 1 + lax.div(me, 2 << section)
        start = lax.rem(lax.div(me, 1 << section), 2) * skel_count
        matrix = top_here[place, pl.ds(pl.multiple_of(start, skel_count), skel_count), :]
        field = times_transposed(field, matrix)
    top_field[...] = field
    lax.fori_loop(7, leaves // 2, two_leaves, 0)
    finish(stage_e)
    target = all_nodes[group, slot][rhs:]
    field = top_field[...]
    for i in range(far_list.shape[1]):
        e = far_list[0, i]
        place = lax.rem(e, wide)
        source = all_nodes[lax.div(e, wide), lax.rem(place, 2) * chips + lax.div(place, 2)]
        field = field + node_field(source, target, rhs)
    fields = [field]
    while len(fields) < leaves:
        parents = len(fields)
        both = [times_transposed(fields[p], transfer_here[parents - 1 + p]) for p in range(parents)]
        fields = [half for pair in both for half in (pair[:, :skel_count], pair[:, skel_count:])]
    scale = 1.0 / math.sqrt(box)
    for leaf in range(leaves):
        far_part = times_transposed(fields[leaf], basis_here[leaf])
        out[leaf] = ((near_out[leaf] + far_part) * scale).astype(BF16)


def shards(
    points, charges, leaf_interp_basis, leaf_skeleton, local_transfer, local_skeleton,
    top_transfer, top_skeleton, near_list, far_list,
):
    points, charges, basis = points[0], charges[0], leaf_interp_basis[0]
    leaves, dims, box = points.shape
    rhs, skel = charges.shape[1], basis.shape[2]
    groups, wide = lax.axis_size("narrow"), lax.axis_size("wide")
    vmem = pl.BlockSpec(memory_space=pltpu.VMEM)
    smem = pl.BlockSpec(memory_space=pltpu.SMEM)
    anywhere = pl.BlockSpec(memory_space=pl.ANY)

    def shape(dtype, *dims):
        return jax.ShapeDtypeStruct(dims, dtype)

    size = (rhs + dims, skel)
    side = math.isqrt(wide // 2)
    copies = 4 + 2 * (side - 1) + 1 + 3 * (groups - 1)
    out = pl.pallas_call(
        main_kernel,
        out_shape=shape(BF16, leaves, rhs, box),
        in_specs=[smem] * 2 + [anywhere] * 5 + [vmem] * 3,
        out_specs=vmem,
        scratch_shapes=[
            pltpu.VMEM((leaves, rhs, box), F32),
            pltpu.VMEM((3, *points.shape), BF16),
            pltpu.VMEM((3 * leaves, rhs, box), BF16),
            pltpu.VMEM(basis.shape, BF16),
            pltpu.VMEM(local_transfer.shape[1:], BF16),
            pltpu.VMEM(top_transfer.shape[1:], BF16),
            pltpu.VMEM((leaves, *size), F32),
            pltpu.VMEM((groups, wide, *size), F32),
            pltpu.VMEM((wide - 1, *size), F32),
            pltpu.VMEM((groups - 1, *size), F32),
            pltpu.VMEM((rhs, skel), F32),
            pltpu.VMEM((3 * leaves, box, 32), BF16),
            pltpu.VMEM((leaves, 32, box), BF16),
            pltpu.VMEM((box, box), BF16),
            pltpu.VMEM((box, box), BF16),
            pltpu.SemaphoreType.DMA((5,)),
            pltpu.SemaphoreType.DMA((copies,)),
            pltpu.SemaphoreType.DMA((copies,)),
        ],
        compiler_params=pltpu.CompilerParams(
            collective_id=0, has_side_effects=True, vmem_limit_bytes=VMEM_BYTES
        ),
        name="main",
    )(
        near_list[0].T, far_list[0], points, charges, basis, local_transfer[0], top_transfer[0],
        leaf_skeleton[0], jnp.swapaxes(local_skeleton, 0, 1), jnp.swapaxes(top_skeleton, 0, 1),
    )
    return out[None]


def solution(mesh):
    return jax.shard_map(
        shards,
        mesh=mesh,
        in_specs=(
            P("narrow", "wide", None, None),
            P("narrow", "wide", None, None),
            P("narrow", "wide", None, None),
            P("narrow", "wide", None),
            P("narrow", "wide", None, None),
            P("narrow", "wide", None),
            P("narrow", None, None, None),
            P("narrow", None, None),
            P("narrow", "wide", None),
            P("narrow", "wide", None),
        ),
        out_specs=P("narrow", "wide", None, None),
        check_vma=False,
    )
```

```python
import functools
import math

import jax
import jax.numpy as jnp
from jax import lax
from jax.experimental import pallas as pl
from jax.experimental.pallas import tpu as pltpu
from jax.sharding import PartitionSpec as P

F32 = jnp.float32
BF16 = jnp.bfloat16
MESH = pl.DeviceIdType.MESH
RATE = 1.5 * math.log2(math.e)
LAST_DIMS = (((1,), (1,)), ((), ()))
FIRST_DIMS = (((0,), (0,)), ((), ()))
VMEM_BYTES = 56 * 2**20
EARLY = 2


def dot(a, b, dims=(((1,), (0,)), ((), ()))):
    return lax.dot_general(a, b, dims, preferred_element_type=F32)


def split3(x):
    first = x.astype(BF16).astype(F32)
    rest = x - first
    second = rest.astype(BF16).astype(F32)
    return first, second, rest - second


def hi_lo(x):
    high = x.astype(BF16)
    return high, (x - high.astype(F32)).astype(BF16)


def tail_rows(parts, slots):
    row = lax.broadcasted_iota(jnp.int32, (8, parts[0].shape[1]), 0)
    ones = (row >= slots[1]) & (row < slots[1] + 3)
    rows = jnp.where(ones, 1.0, 0.0)
    for i, part in enumerate(parts):
        rows = jnp.where(row == slots[0] + i, part, rows)
    return rows


def source_rows(points):
    norm = -RATE * jnp.sum(points * points, axis=0, keepdims=True)
    return jnp.concatenate([*split3(2.0 * RATE * points), tail_rows(split3(norm), (0, 3))], axis=0)


def target_rows(points):
    norm = -RATE * jnp.sum(points * points, axis=0, keepdims=True)
    return jnp.concatenate([points, points, points, tail_rows(split3(norm), (3, 0))], axis=0)


def merge(left, right, transfer, chosen, rhs):
    skel = left.shape[1]
    joined = jnp.concatenate([left, right], axis=1)
    high, low = hi_lo(joined[:rhs])
    rows = jnp.concatenate([high, low, joined[rhs:].astype(BF16)], axis=0)
    index = lax.broadcasted_iota(jnp.int32, (2 * skel, skel), 0)
    table = jnp.where(index == chosen, 1.0, 0.0).astype(BF16)
    both = dot(rows, jnp.concatenate([transfer, table], axis=1))
    weight = both[:rhs, :skel] + both[rhs : 2 * rhs, :skel]
    return jnp.concatenate([weight, both[2 * rhs :, skel:]], axis=0)


def node_field(source, target, rhs):
    log_kernel = dot(
        source_rows(source[rhs:]).astype(BF16), target_rows(target).astype(BF16), FIRST_DIMS
    )
    kernel_high, kernel_low = hi_lo(jnp.exp2(log_kernel))
    high, low = hi_lo(source[:rhs])
    both = dot(jnp.concatenate([high, low], axis=0), kernel_high)
    return both[:rhs] + both[rhs:] + dot(high, kernel_low)


def times_transposed(field, matrix):
    rows = field.shape[0]
    both = dot(jnp.concatenate(hi_lo(field), axis=0), matrix, LAST_DIMS)
    return both[:rows] + both[rows:]


def main_kernel(
    near_list, far_list, points, charges, basis, transfer, top_transfer, leaf_skel, skel, top_skel,
    out,
    near_out, near_points, near_charges, basis_here, transfer_here, top_here, nodes, all_nodes, tree, roots, top_field,
    sources, targets, kernel_a, kernel_b, early, local_sem, send_sem, recv_sem,
):
    leaves, rhs, box = charges.shape
    skel_count = basis.shape[2]
    near = near_list.shape[0]
    wide, groups = lax.axis_size("wide"), lax.axis_size("narrow")
    me, group = lax.axis_index("wide"), lax.axis_index("narrow")
    chips = wide // 2
    side = math.isqrt(chips)
    core, chip = lax.rem(me, 2), lax.div(me, 2)
    row, column = lax.div(chip, side), lax.rem(chip, side)
    right, left = lax.rem(me + 1, wide), lax.rem(me + wide - 1, wide)
    sibling = chip * 2 + 1 - core

    def in_row(step):
        return lax.rem(column + step, side)

    def in_column(step):
        return lax.rem(row + step, side)

    def in_groups(step):
        return lax.rem(group + step, groups)

    row_peers = [(row * side + in_row(d)) * 2 + core for d in range(1, side)]
    column_peers = [(in_column(d) * side + column) * 2 + core for d in range(1, side)]
    group_peers = [in_groups(d) for d in range(1, groups)]

    local = [
        pltpu.make_async_copy(src, dst, local_sem.at[i])
        for i, (src, dst) in enumerate(
            (
                (charges, near_charges.at[pl.ds(leaves, leaves)]),
                (points, near_points.at[1]),
                (basis, basis_here),
                (transfer, transfer_here),
                (top_transfer, top_here),
            )
        )
    ]
    for copy in local:
        copy.start()
    barrier = pltpu.get_barrier_semaphore()
    wide_peers = [right, left] + row_peers + column_peers
    for other in wide_peers:
        pl.semaphore_signal(barrier, inc=1, device_id={"wide": other}, device_id_type=MESH)
    for other in group_peers:
        pl.semaphore_signal(barrier, inc=1, device_id={"narrow": other}, device_id_type=MESH)
    pl.semaphore_wait(barrier, len(wide_peers) + len(group_peers))

    used = []

    def exchange(src, dst, device, incoming=None):
        i = len(used)
        used.append(i)
        sems = {"send_sem": send_sem.at[i], "recv_sem": recv_sem.at[i]}
        sent = pltpu.make_async_remote_copy(
            src_ref=src, dst_ref=dst, device_id=device, device_id_type=MESH, **sems
        )
        landed = dst if incoming is None else incoming
        got = pltpu.make_async_remote_copy(
            src_ref=landed, dst_ref=landed, device_id=device, device_id_type=MESH, **sems
        )
        sent.start()
        return sent, got

    def finish(pairs):
        for sent, got in pairs:
            sent.wait_send()
            got.wait_recv()

    sides = ((right, 0), (left, 2))
    halo_points = [exchange(points, near_points.at[b], {"wide": other}) for other, b in sides]
    halo_charges = [
        exchange(charges, near_charges.at[pl.ds(b * leaves, leaves)], {"wide": other})
        for other, b in sides
    ]

    for copy in local[:3]:
        copy.wait()
    step = 4

    def leaf_nodes(first, carry):
        for leaf in [first * step + i for i in range(step)]:
            spots = near_points[1, leaf]
            index = lax.broadcasted_iota(jnp.int32, (box, skel_count), 0)
            table = jnp.where(index == leaf_skel[pl.ds(leaf, 1), :], 1.0, 0.0).astype(BF16)
            weight = dot(near_charges[leaves + leaf], basis_here[leaf])
            coords = dot(spots, table)
            nodes[leaf] = jnp.concatenate([weight, coords], axis=0)
        return carry

    lax.fori_loop(0, leaves // step, leaf_nodes, 0)
    local[3].wait()
    level = [nodes[leaf] for leaf in range(leaves)]
    while len(level) > 1:
        parents = len(level) // 2
        level = [
            merge(
                level[2 * p], level[2 * p + 1], transfer_here[parents - 1 + p],
                skel[parents - 1 + p], rhs,
            )
            for p in range(parents)
        ]
    half = core * chips
    slot = half + chip
    all_nodes[group, slot] = level[0]
    mine = all_nodes.at[group, slot]
    stage_a = [
        exchange(
            mine, mine, {"wide": other},
            all_nodes.at[group, half + row * side + in_row(side - d)],
        )
        for d, other in enumerate(row_peers, 1)
    ]


    def fill_own(leaf, buffer):
        spots = near_points[1, leaf].astype(F32)
        source = source_rows(spots).T.astype(BF16)
        target = target_rows(spots).astype(BF16)
        sources[leaves + leaf] = source
        targets[leaf] = target
        buffer[...] = jnp.exp2(dot(source, target)).astype(BF16)

    def own_pair(pair, carry):
        for i, (now, later) in enumerate(((kernel_a, kernel_b), (kernel_b, kernel_a))):
            leaf = 2 * pair + i
            fill_own(lax.rem(leaf + 1, leaves), later)
            near_out[leaf] = dot(near_charges[leaves + leaf], now[...])
        return carry

    def own_pair_and_halo(pair, carry):
        own_pair(pair, carry)
        for leaf in [(pair - leaves // 4) * 4 + i for i in range(4)]:
            for block in (0, 2):
                spots = near_points[block, leaf].astype(F32)
                sources[block * leaves + leaf] = source_rows(spots).T.astype(BF16)
        return carry

    fill_own(0, kernel_a)
    lax.fori_loop(0, leaves // 4, own_pair, 0)
    finish(halo_points)
    lax.fori_loop(leaves // 4, leaves // 2, own_pair_and_halo, 0)
    first_leaf = (me - 1) * leaves

    def place_of(leaf, k):
        return jnp.clip(near_list[k, leaf] - first_leaf, 0, 3 * leaves - 1)

    def fill(leaf, k, buffer):
        source = sources[place_of(leaf, k)]
        buffer[...] = jnp.exp2(dot(source, targets[leaf])).astype(BF16)

    def two_leaves(pair, carry):
        steps = [(2 * pair + i, k) for i in range(2) for k in range(1, near)]
        steps.append((lax.rem(2 * pair + 2, leaves), 1))
        total = None
        for i, (leaf, k) in enumerate(steps[:-1]):
            now, later = (kernel_a, kernel_b) if i % 2 == 0 else (kernel_b, kernel_a)
            fill(*steps[i + 1], later)
            part = dot(near_charges[place_of(leaf, k)], now[...])
            total = (near_out[leaf] if k == 1 else total) + part
            if k == near - 1:
                near_out[leaf] = total
        return carry

    def fill_leaf(leaf, carry):
        for k in range(1, near):
            fill(leaf, k, early.at[leaf * (near - 1) + k - 1])
        return carry

    def use_leaf(leaf, carry):
        total = near_out[leaf]
        for k in range(1, near):
            block = early[leaf * (near - 1) + k - 1]
            total = total + dot(near_charges[place_of(leaf, k)], block)
        near_out[leaf] = total
        return carry

    lax.fori_loop(0, EARLY, fill_leaf, 0)
    finish(stage_a)
    line = all_nodes.at[group, pl.ds(half + row * side, side)]
    stage_b = [
        exchange(
            line, line, {"wide": other},
            all_nodes.at[group, pl.ds(half + in_column(side - d) * side, side)],
        )
        for d, other in enumerate(column_peers, 1)
    ]
    finish(halo_charges)
    lax.fori_loop(0, EARLY, use_leaf, 0)
    fill(EARLY, 1, kernel_a)
    lax.fori_loop(EARLY // 2, 2, two_leaves, 0)
    finish(stage_b)
    plane = all_nodes.at[group, pl.ds(half, chips)]
    other_half = pl.ds((1 - core) * chips, chips)
    stage_d = [
        exchange(
            plane, plane, {"narrow": other},
            all_nodes.at[in_groups(groups - d), pl.ds(half, chips)],
        )
        for d, other in enumerate(group_peers, 1)
    ]
    stage_c = [exchange(plane, plane, {"wide": sibling}, all_nodes.at[group, other_half])]
    lax.fori_loop(2, 4, two_leaves, 0)
    finish(stage_c)
    local[4].wait()

    parents = chips
    while parents >= 1:
        step = min(4, parents)
        base = parents - 1

        def level(first, carry, step=step, base=base, parents=parents):
            for p in [first * step + i for i in range(step)]:
                if parents == chips:
                    left, right = all_nodes[group, p], all_nodes[group, chips + p]
                else:
                    left, right = tree[2 * base + 1 + 2 * p], tree[2 * base + 2 + 2 * p]
                tree[base + p] = merge(left, right, top_here[base + p], top_skel[base + p], rhs)
            return carry

        if step == parents:
            level(0, 0)
        else:
            lax.fori_loop(0, parents // step, level, 0)
        parents //= 2
    stage_r = [
        exchange(tree.at[0], roots.at[d], {"narrow": other}) for d, other in enumerate(group_peers)
    ]

    def pass_on(d):
        other = in_groups(groups - d)
        block = all_nodes.at[other, pl.ds(half, chips)]
        mirrored = all_nodes.at[other, other_half]
        return exchange(block, block, {"wide": sibling}, mirrored)

    lax.fori_loop(4, 7, two_leaves, 0)
    finish(stage_d)
    stage_e = [pass_on(d) for d in range(1, groups)]
    finish(stage_r)
    target = tree[0][rhs:]
    field = None
    for i in range(groups - 1):
        part = node_field(roots[i], target, rhs)
        field = part if field is None else field + part
    for section in reversed(range(wide.bit_length() - 1)):
        place = (wide >> section + 1) - 1 + lax.div(me, 2 << section)
        start = lax.rem(lax.div(me, 1 << section), 2) * skel_count
        matrix = top_here[place, pl.ds(pl.multiple_of(start, skel_count), skel_count), :]
        field = times_transposed(field, matrix)
    top_field[...] = field
    lax.fori_loop(7, leaves // 2, two_leaves, 0)
    finish(stage_e)
    target = all_nodes[group, slot][rhs:]
    field = top_field[...]
    for i in range(far_list.shape[1]):
        e = far_list[0, i]
        place = lax.rem(e, wide)
        source = all_nodes[lax.div(e, wide), lax.rem(place, 2) * chips + lax.div(place, 2)]
        field = field + node_field(source, target, rhs)
    fields = [field]
    while len(fields) < leaves:
        parents = len(fields)
        both = [times_transposed(fields[p], transfer_here[parents - 1 + p]) for p in range(parents)]
        fields = [half for pair in both for half in (pair[:, :skel_count], pair[:, skel_count:])]
    scale = 1.0 / math.sqrt(box)
    for leaf in range(leaves):
        far_part = times_transposed(fields[leaf], basis_here[leaf])
        out[leaf] = ((near_out[leaf] + far_part) * scale).astype(BF16)


def shards(
    points, charges, leaf_interp_basis, leaf_skeleton, local_transfer, local_skeleton,
    top_transfer, top_skeleton, near_list, far_list,
):
    points, charges, basis = points[0], charges[0], leaf_interp_basis[0]
    leaves, dims, box = points.shape
    rhs, skel = charges.shape[1], basis.shape[2]
    groups, wide = lax.axis_size("narrow"), lax.axis_size("wide")
    vmem = pl.BlockSpec(memory_space=pltpu.VMEM)
    smem = pl.BlockSpec(memory_space=pltpu.SMEM)
    anywhere = pl.BlockSpec(memory_space=pl.ANY)

    def shape(dtype, *dims):
        return jax.ShapeDtypeStruct(dims, dtype)

    size = (rhs + dims, skel)
    side = math.isqrt(wide // 2)
    copies = 4 + 2 * (side - 1) + 1 + 3 * (groups - 1)
    out = pl.pallas_call(
        main_kernel,
        out_shape=shape(BF16, leaves, rhs, box),
        in_specs=[smem] * 2 + [anywhere] * 5 + [vmem] * 3,
        out_specs=vmem,
        scratch_shapes=[
            pltpu.VMEM((leaves, rhs, box), F32),
            pltpu.VMEM((3, *points.shape), BF16),
            pltpu.VMEM((3 * leaves, rhs, box), BF16),
            pltpu.VMEM(basis.shape, BF16),
            pltpu.VMEM(local_transfer.shape[1:], BF16),
            pltpu.VMEM(top_transfer.shape[1:], BF16),
            pltpu.VMEM((leaves, *size), F32),
            pltpu.VMEM((groups, wide, *size), F32),
            pltpu.VMEM((wide - 1, *size), F32),
            pltpu.VMEM((groups - 1, *size), F32),
            pltpu.VMEM((rhs, skel), F32),
            pltpu.VMEM((3 * leaves, box, 32), BF16),
            pltpu.VMEM((leaves, 32, box), BF16),
            pltpu.VMEM((box, box), BF16),
            pltpu.VMEM((box, box), BF16),
            pltpu.VMEM((EARLY * (near_list.shape[2] - 1), box, box), BF16),
            pltpu.SemaphoreType.DMA((5,)),
            pltpu.SemaphoreType.DMA((copies,)),
            pltpu.SemaphoreType.DMA((copies,)),
        ],
        compiler_params=pltpu.CompilerParams(
            collective_id=0, has_side_effects=True, vmem_limit_bytes=VMEM_BYTES
        ),
        name="main",
    )(
        near_list[0].T, far_list[0], points, charges, basis, local_transfer[0], top_transfer[0],
        leaf_skeleton[0], jnp.swapaxes(local_skeleton, 0, 1), jnp.swapaxes(top_skeleton, 0, 1),
    )
    return out[None]


def solution(mesh):
    return jax.shard_map(
        shards,
        mesh=mesh,
        in_specs=(
            P("narrow", "wide", None, None),
            P("narrow", "wide", None, None),
            P("narrow", "wide", None, None),
            P("narrow", "wide", None),
            P("narrow", "wide", None, None),
            P("narrow", "wide", None),
            P("narrow", None, None, None),
            P("narrow", None, None),
            P("narrow", "wide", None),
            P("narrow", "wide", None),
        ),
        out_specs=P("narrow", "wide", None, None),
        check_vma=False,
    )
```
